32 devices in a mesh: rows: 16 (over z, y, x), cols: 2 (over core).
Axes of the slice: x: 2, y: 2, z: 4, core: 2. Of those that a mesh axis runs over, the one named last changes fastest.
Arguments:
- points: float32 [8192, 768], P('rows'), may hold values from -83 to 83
- landmark_index: int32 [4096], P('rows'), may hold values from 0 to 8191, as said below
- targets: float32 [4096, 512], P('rows', 'cols'), may hold values from -6 to 6
- ridge_shift: float32 [1], replicated, may hold values from 0.5 to 2
Outputs:
- projected: float32 [512, 2048], P('rows', 'cols')
- panels: float32 [4096, 256], P('rows')
- remainder: float32 [4096, 1792], P('rows', 'cols')
The draws below stay inside these ranges and needn't reach their ends.
Inputs may be any that keep to these rules, and one draw needn't show every extreme that they name: `landmark_index`: landmark i is a point of the block [(i // 256) * 512, (i // 256 + 1) * 512); the 256 landmarks of one block are distinct.
All inputs are finite; a program needn't handle non-finite values.
Results may differ from the reference program's by a relative error of at most 0.00028.
Values sent between devices are 32-bit elements; how exact they have to be, the bound alone decides.
A program may use at most 64 MiB of HBM per device.

```python
import math
import jax
import jax.numpy as jnp
from jax import lax

E = 768
C = 2048
R = 512
PW = 128
L_DEV = 256
P_DEV = 512
LANDMARKS = 4096
POINTS = 8192
N_ROWS = 16


def draw_landmark_index(key, part):
    blocks = LANDMARKS // L_DEV
    block_keys = jax.random.split(jax.random.fold_in(key, 17), blocks)
    chosen = jax.vmap(lambda block_key: jax.random.permutation(block_key, P_DEV)[:L_DEV])(block_keys)
    shifted = chosen + (jnp.arange(blocks, dtype=jnp.int32) * P_DEV)[:, None]
    return shifted.reshape(-1).astype(jnp.int32)


def draw_points(key, part):
    base_key = jax.random.fold_in(key, 29)
    latent_key, mapping_key, perturb_key = jax.random.split(base_key, 3)
    mapping = jnp.clip(jax.random.normal(mapping_key, (8, E), jnp.float32) * math.sqrt(3.0 / 8.0), -2.5, 2.5)
    latent = jnp.clip(jax.random.normal(latent_key, (POINTS, 8), jnp.float32), -4.0, 4.0)
    perturb = 0.3 * jnp.clip(jax.random.normal(perturb_key, (POINTS, E), jnp.float32), -4.0, 4.0)
    mapped = jnp.dot(latent, mapping, precision=lax.Precision.HIGHEST, preferred_element_type=jnp.float32)
    return (mapped + perturb).astype(jnp.float32)


def steps_of(stream_key, dims, pieces, smallest, high):
    gain = 1.0
    for position, blocks in pieces:
        heights = jax.random.uniform(jax.random.fold_in(jax.random.fold_in(stream_key, 6), position), (blocks,), jnp.float32, smallest / len(pieces), high / len(pieces))
        gain = gain * jnp.repeat(jnp.exp(heights), dims[position] // blocks).reshape((-1,) + (1,) * (len(dims) - 1 - position))
    return gain


def centred(rng, extent, scale, most, shards=(), kind=jnp.bfloat16):
    drawn = scale * jax.random.normal(rng, extent, jnp.float32)
    if shards:
        drawn = drawn * steps_of(rng, extent, shards, -0.22, 0.18)
    return jnp.clip(drawn, -most, most).astype(kind)


def setup_inputs(seed: int = 0) -> dict:
    splits = jax.random.split(jax.random.key(seed), 5)
    return {
        "points": draw_points(jax.random.fold_in(splits[4], 71), 0),
        "landmark_index": draw_landmark_index(jax.random.fold_in(splits[4], 71), 0),
        "targets": centred(splits[2], (LANDMARKS, R), 1.0, 6.0, ((0, 16), (1, 2)), jnp.float32),
        "ridge_shift": jnp.clip(jnp.exp(jax.random.uniform(splits[3], (1,), jnp.float32, math.log(0.5), math.log(2.0))), 0.5, 2.0),
    }


exact_mode = lax.Precision.HIGHEST

def gaussian(left_rows, right_rows):
    left_sq = jnp.sum(left_rows * left_rows, axis=1)
    right_sq = jnp.sum(right_rows * right_rows, axis=1)
    cross_term = jnp.dot(left_rows.astype(jnp.float32), right_rows.T.astype(jnp.float32), precision=exact_mode, preferred_element_type=jnp.float32)
    return jnp.exp(-(left_sq[:, None] + right_sq[None, :] - 2.0 * cross_term) / (2.0 * left_rows.shape[1]))

def reference(points, landmark_index, targets, ridge_shift):
    embedded = points[landmark_index]
    half_cols = C // 2
    quarter = half_cols // N_ROWS
    column_ids = jnp.arange(C, dtype=jnp.int32)
    within = column_ids % half_cols
    land_cols = within // quarter * L_DEV + column_ids // half_cols * quarter + within % quarter
    column_emb = embedded[land_cols]
    row_ids = jnp.arange(embedded.shape[0], dtype=jnp.int32)
    kernel_slab = gaussian(embedded, column_emb) + jnp.where(row_ids[:, None] == land_cols[None, :], ridge_shift[0], 0.0)
    projected = lax.dot_general(targets.astype(jnp.float32), kernel_slab.astype(jnp.float32), (((0,), (0,)), ((), ())), precision=exact_mode, preferred_element_type=jnp.float32)
    panel_list = []
    for first_col in (0, half_cols):
        panel_cols = kernel_slab[:, first_col:first_col + PW]
        diag_block = panel_cols[land_cols[first_col:first_col + PW]]
        factor = jnp.linalg.cholesky(diag_block)
        local_panel = jax.scipy.linalg.solve_triangular(factor, panel_cols.T, lower=True).T
        kernel_slab = kernel_slab - jnp.dot(local_panel.astype(jnp.float32), local_panel[land_cols].T.astype(jnp.float32), precision=exact_mode, preferred_element_type=jnp.float32)
        panel_list.append(local_panel)
    remainder = jnp.concatenate([kernel_slab[:, PW:half_cols], kernel_slab[:, half_cols + PW:]], axis=1)
    return (projected, jnp.concatenate(panel_list, axis=1), remainder)
```

```python
import jax
import jax.numpy as jnp
from jax import lax
from jax.sharding import PartitionSpec as P

C = 2048
PW = 128

exact_mode = lax.Precision.HIGHEST


def dot_t(left, right):
    return lax.dot_general(
        left, right, (((1,), (1,)), ((), ())), precision=exact_mode, preferred_element_type=jnp.float32
    )


def gaussian(left_rows, right_rows):
    left_sq = jnp.sum(left_rows * left_rows, axis=1)
    right_sq = jnp.sum(right_rows * right_rows, axis=1)
    cross_term = dot_t(left_rows, right_rows)
    return jnp.exp(
        -(left_sq[:, None] + right_sq[None, :] - 2.0 * cross_term) / (2.0 * left_rows.shape[1])
    )


def inverse_factor(block):
    factor = jnp.linalg.cholesky(block)
    eye = jnp.eye(block.shape[0], dtype=jnp.float32)
    return jax.scipy.linalg.solve_triangular(factor, eye, lower=True)


def per_device(points, landmark_index, targets, ridge_shift):
    rows_here = landmark_index.shape[0]
    block_points = points.shape[0]
    row_pos = lax.axis_index("rows")
    col_pos = lax.axis_index("cols")
    n_rows = lax.axis_size("rows")
    half_cols = C // 2
    quarter = half_cols // n_rows
    ridge = ridge_shift[0]
    local_index = landmark_index - row_pos * block_points
    embedded = jnp.take(points, local_index, axis=0)
    own_landmarks = lax.dynamic_slice_in_dim(embedded, col_pos * quarter, quarter, 0)
    column_emb = lax.all_gather(own_landmarks, "rows", axis=0, tiled=True)
    heads = lax.all_gather(column_emb[:PW], "cols", axis=0, tiled=True)
    all_targets = lax.all_gather(targets, "cols", axis=1, tiled=True)

    row_ids = lax.broadcasted_iota(jnp.int32, (rows_here, half_cols), 0)
    col_ids = lax.broadcasted_iota(jnp.int32, (rows_here, half_cols), 1)
    offset = row_ids - col_pos * quarter
    ridge_hits = (offset >= 0) & (offset < quarter) & (col_ids == row_pos * quarter + offset)
    kernel_slab = gaussian(embedded, column_emb) + jnp.where(ridge_hits, ridge, 0.0)
    projected = lax.psum_scatter(
        lax.dot_general(
            all_targets,
            kernel_slab,
            (((0,), (0,)), ((), ())),
            precision=exact_mode,
            preferred_element_type=jnp.float32,
        ),
        "rows",
        scatter_dimension=0,
        tiled=True,
    )

    base = gaussian(heads, heads) + ridge * jnp.eye(2 * PW, dtype=jnp.float32)
    inv0 = inverse_factor(base[:PW, :PW])
    low = dot_t(base[PW:, :PW], inv0)
    inv1 = inverse_factor(base[PW:, PW:] - dot_t(low, low))

    hrow = lax.broadcasted_iota(jnp.int32, (rows_here, 2 * PW), 0)
    hcol = lax.broadcasted_iota(jnp.int32, (rows_here, 2 * PW), 1)
    hblock = hcol // PW
    hoff = hrow - hblock * quarter
    head_hits = (hoff >= 0) & (hoff < quarter) & (hcol - hblock * PW == row_pos * quarter + hoff)
    head_slab = gaussian(embedded, heads) + jnp.where(head_hits, ridge, 0.0)

    lrow = lax.broadcasted_iota(jnp.int32, (half_cols, 2 * PW), 0)
    lcol = lax.broadcasted_iota(jnp.int32, (half_cols, 2 * PW), 1)
    land_slab = gaussian(column_emb, heads) + jnp.where(
        (lrow < PW) & (lcol == col_pos * PW + lrow), ridge, 0.0
    )

    def panels_of(slab):
        first = dot_t(slab[:, :PW], inv0)
        second = dot_t(slab[:, PW:] - dot_t(first, low), inv1)
        return jnp.concatenate([first, second], axis=1)

    panels = panels_of(head_slab)
    land_panels = panels_of(land_slab)
    remainder = kernel_slab[:, PW:] - dot_t(panels, land_panels[PW:])
    return (projected, panels, remainder)


def solution(mesh):
    in_specs = (P("rows", None), P("rows"), P("rows", "cols"), P())
    out_specs = (P("rows", "cols"), P("rows", None), P("rows", "cols"))
    return jax.shard_map(
        per_device, mesh=mesh, in_specs=in_specs, out_specs=out_specs, check_vma=False
    )
```

```python
import jax
import jax.numpy as jnp
from jax import lax
from jax.experimental import pallas as pl
from jax.experimental.pallas import tpu as pltpu
from jax.sharding import PartitionSpec as P

C = 2048
PW = 128

exact_mode = lax.Precision.HIGHEST


def dot_t(left, right):
    return lax.dot_general(
        left, right, (((1,), (1,)), ((), ())), precision=exact_mode, preferred_element_type=jnp.float32
    )


def gaussian(left_rows, right_rows):
    left_sq = jnp.sum(left_rows * left_rows, axis=1)
    right_sq = jnp.sum(right_rows * right_rows, axis=1)
    cross_term = dot_t(left_rows, right_rows)
    return jnp.exp(
        -(left_sq[:, None] + right_sq[None, :] - 2.0 * cross_term) / (2.0 * left_rows.shape[1])
    )


def inverse_factor(block):
    factor = jnp.linalg.cholesky(block)
    eye = jnp.eye(block.shape[0], dtype=jnp.float32)
    return jax.scipy.linalg.solve_triangular(factor, eye, lower=True)


MESH = pl.DeviceIdType.MESH
PLANE = 4


def gather_kernel(emb_ref, tgt_ref, col_ref, head_ref, all_tgt_ref, send, recv):
    r = lax.axis_index("rows")
    c = lax.axis_index("cols")
    n_rows = lax.axis_size("rows")
    lines = n_rows // PLANE
    line, q = r // PLANE, r % PLANE
    quarter = col_ref.shape[0] // n_rows
    half = col_ref.shape[1] // 2
    x = line * PLANE + (q + 1 - 2 * (q % 2))
    y = line * PLANE + (q + 2) % PLANE
    qx, qy = q + 1 - 2 * (q % 2), (q + 2) % PLANE
    up, down = r + PLANE, r - PLANE
    has_up, has_down = line < lines - 1, line > 0
    core = (r, 1 - c)

    def rows_of(t, who):
        return pl.ds(pl.multiple_of((t * PLANE + who) * quarter, quarter), quarter)

    own = emb_ref.at[pl.ds(pl.multiple_of(c * quarter, quarter), quarter)]

    def remote(src, dst, kind, t, dev):
        return pltpu.make_async_remote_copy(
            src_ref=src, dst_ref=dst, send_sem=send.at[kind, t], recv_sem=recv.at[kind, t],
            device_id=dev, device_id_type=MESH,
        )

    def whole(kind, t, who, dev, first=False):
        dst = col_ref.at[rows_of(t, who)]
        return remote(own if first else dst, dst, kind, t, dev)

    def part(kind, t, who, side, dev):
        dst = col_ref.at[rows_of(t, who), pl.ds(side * half, half)]
        return remote(dst, dst, kind, t, dev)

    barrier = pltpu.get_barrier_semaphore()
    for dev in ((x, c), (y, c), core):
        pl.semaphore_signal(barrier, inc=1, device_id=dev, device_id_type=MESH)

    @pl.when(has_up)
    def _():
        pl.semaphore_signal(barrier, inc=1, device_id=(up, c), device_id_type=MESH)

    @pl.when(has_down)
    def _():
        pl.semaphore_signal(barrier, inc=1, device_id=(down, c), device_id_type=MESH)

    pl.semaphore_wait(barrier, 3 + jnp.where(has_up, 1, 0) + jnp.where(has_down, 1, 0))

    def send_on(t, first=False):
        whole(2, t, q, (x, c), first).start()
        whole(3, t, q, (y, c), first).start()

    own_copy = pltpu.make_async_copy(own, col_ref.at[rows_of(line, q)], send.at[7, 0])
    tgt_copy = pltpu.make_async_copy(tgt_ref, all_tgt_ref.at[c], send.at[7, 1])

    @pl.when(has_up)
    def _():
        whole(0, line, q, (up, c), True).start()

    @pl.when(has_down)
    def _():
        whole(1, line, q, (down, c), True).start()

    send_on(line, True)
    own_copy.start()
    tgt_copy.start()
    tgt_swap = remote(tgt_ref, all_tgt_ref.at[c], 6, 0, core)
    tgt_swap.start()

    def ring_stage(t):
        whole(2, t, qx, (x, c)).wait_recv()
        part(5, t, qx, 0, (y, c)).start()
        whole(3, t, qy, (y, c)).wait_recv()
        part(4, t, qy, 1, (x, c)).start()

    for step in range(1, lines + 1):
        if step < lines:
            @pl.when(line - step >= 0)
            def _(step=step):
                t = line - step
                whole(0, t, q, (up, c)).wait_recv()

                @pl.when(has_up)
                def _():
                    whole(0, t, q, (up, c)).start()

                send_on(t)

            @pl.when(line + step < lines)
            def _(step=step):
                t = line + step
                whole(1, t, q, (down, c)).wait_recv()

                @pl.when(has_down)
                def _():
                    whole(1, t, q, (down, c)).start()

                send_on(t)

        if step == 1:
            ring_stage(line)
        else:
            @pl.when(line - (step - 1) >= 0)
            def _(step=step):
                ring_stage(line - (step - 1))

            @pl.when(line + (step - 1) < lines)
            def _(step=step):
                ring_stage(line + (step - 1))

    opposite = (q + 2 - 4 * (q // 2)) + 1 - 2 * (q % 2)
    for t in range(lines):
        part(4, t, opposite, 1, (x, c)).wait_recv()
        part(5, t, opposite, 0, (y, c)).wait_recv()
    own_copy.wait()

    heads = col_ref.at[pl.ds(0, PW)]
    head_copy = pltpu.make_async_copy(heads, head_ref.at[c], send.at[7, 2])
    head_swap = remote(heads, head_ref.at[c], 6, 1, core)
    head_copy.start()
    head_swap.start()

    for t in range(lines):
        whole(2, t, q, (x, c)).wait_send()
        whole(3, t, q, (y, c)).wait_send()
        part(4, t, qy, 1, (x, c)).wait_send()
        part(5, t, qx, 0, (y, c)).wait_send()

        @pl.when(has_up & (t <= line))
        def _(t=t):
            whole(0, t, q, (up, c)).wait_send()

        @pl.when(has_down & (t >= line))
        def _(t=t):
            whole(1, t, q, (down, c)).wait_send()

    tgt_copy.wait()
    head_copy.wait()
    remote(tgt_ref, all_tgt_ref.at[1 - c], 6, 0, core).wait()
    remote(heads, head_ref.at[1 - c], 6, 1, core).wait()


def gather(embedded, targets, n_rows):
    width = embedded.shape[1]
    return pl.pallas_call(
        gather_kernel,
        out_shape=(
            jax.ShapeDtypeStruct((C // 2, width), jnp.float32),
            jax.ShapeDtypeStruct((2, PW, width), jnp.float32),
            jax.ShapeDtypeStruct((2,) + targets.shape, jnp.float32),
        ),
        in_specs=[pl.BlockSpec(memory_space=pl.ANY)] * 2,
        out_specs=(pl.BlockSpec(memory_space=pl.ANY),) * 3,
        scratch_shapes=[
            pltpu.SemaphoreType.DMA((8, max(n_rows // PLANE, 3))),
            pltpu.SemaphoreType.DMA((8, max(n_rows // PLANE, 3))),
        ],
        compiler_params=pltpu.CompilerParams(collective_id=0, has_side_effects=True),
    )(embedded, targets)


def per_device(points, landmark_index, targets, ridge_shift):
    rows_here = landmark_index.shape[0]
    block_points = points.shape[0]
    row_pos = lax.axis_index("rows")
    col_pos = lax.axis_index("cols")
    n_rows = lax.axis_size("rows")
    half_cols = C // 2
    quarter = half_cols // n_rows
    ridge = ridge_shift[0]
    local_index = landmark_index - row_pos * block_points
    embedded = jnp.take(points, local_index, axis=0)
    column_emb, head_pair, target_pair = gather(embedded, targets, n_rows)
    heads = head_pair.reshape(2 * PW, -1)
    all_targets = jnp.concatenate([target_pair[0], target_pair[1]], axis=1)

    row_ids = lax.broadcasted_iota(jnp.int32, (rows_here, half_cols), 0)
    col_ids = lax.broadcasted_iota(jnp.int32, (rows_here, half_cols), 1)
    offset = row_ids - col_pos * quarter
    ridge_hits = (offset >= 0) & (offset < quarter) & (col_ids == row_pos * quarter + offset)
    kernel_slab = gaussian(embedded, column_emb) + jnp.where(ridge_hits, ridge, 0.0)
    projected = lax.psum_scatter(
        lax.dot_general(
            all_targets,
            kernel_slab,
            (((0,), (0,)), ((), ())),
            precision=exact_mode,
            preferred_element_type=jnp.float32,
        ),
        "rows",
        scatter_dimension=0,
        tiled=True,
    )

    base = gaussian(heads, heads) + ridge * jnp.eye(2 * PW, dtype=jnp.float32)
    inv0 = inverse_factor(base[:PW, :PW])
    low = dot_t(base[PW:, :PW], inv0)
    inv1 = inverse_factor(base[PW:, PW:] - dot_t(low, low))

    hrow = lax.broadcasted_iota(jnp.int32, (rows_here, 2 * PW), 0)
    hcol = lax.broadcasted_iota(jnp.int32, (rows_here, 2 * PW), 1)
    hblock = hcol // PW
    hoff = hrow - hblock * quarter
    head_hits = (hoff >= 0) & (hoff < quarter) & (hcol - hblock * PW == row_pos * quarter + hoff)
    head_slab = gaussian(embedded, heads) + jnp.where(head_hits, ridge, 0.0)

    lrow = lax.broadcasted_iota(jnp.int32, (half_cols, 2 * PW), 0)
    lcol = lax.broadcasted_iota(jnp.int32, (half_cols, 2 * PW), 1)
    land_slab = gaussian(column_emb, heads) + jnp.where(
        (lrow < PW) & (lcol == col_pos * PW + lrow), ridge, 0.0
    )

    def panels_of(slab):
        first = dot_t(slab[:, :PW], inv0)
        second = dot_t(slab[:, PW:] - dot_t(first, low), inv1)
        return jnp.concatenate([first, second], axis=1)

    panels = panels_of(head_slab)
    land_panels = panels_of(land_slab)
    remainder = kernel_slab[:, PW:] - dot_t(panels, land_panels[PW:])
    return (projected, panels, remainder)


def solution(mesh):
    in_specs = (P("rows", None), P("rows"), P("rows", "cols"), P())
    out_specs = (P("rows", "cols"), P("rows", None), P("rows", "cols"))
    return jax.shard_map(
        per_device, mesh=mesh, in_specs=in_specs, out_specs=out_specs, check_vma=False
    )
```

```python
import jax
import jax.numpy as jnp
from jax import lax
from jax.experimental import pallas as pl
from jax.experimental.pallas import tpu as pltpu
from jax.sharding import PartitionSpec as P

C = 2048
PW = 128
BLOCK = 32

exact_mode = lax.Precision.HIGHEST


def dot_t(left, right):
    return lax.dot_general(
        left, right, (((1,), (1,)), ((), ())), precision=exact_mode, preferred_element_type=jnp.float32
    )


def gaussian(left_rows, right_rows):
    left_sq = jnp.sum(left_rows * left_rows, axis=1)
    right_sq = jnp.sum(right_rows * right_rows, axis=1)
    cross_term = dot_t(left_rows, right_rows)
    return jnp.exp(
        -(left_sq[:, None] + right_sq[None, :] - 2.0 * cross_term) / (2.0 * left_rows.shape[1])
    )


MESH = pl.DeviceIdType.MESH
PLANE = 4


def gather_kernel(emb_ref, tgt_ref, col_ref, head_ref, all_tgt_ref, send, recv):
    r = lax.axis_index("rows")
    c = lax.axis_index("cols")
    n_rows = lax.axis_size("rows")
    lines = n_rows // PLANE
    line, q = r // PLANE, r % PLANE
    quarter = col_ref.shape[0] // n_rows
    half = col_ref.shape[1] // 2
    x = line * PLANE + (q + 1 - 2 * (q % 2))
    y = line * PLANE + (q + 2) % PLANE
    qx, qy = q + 1 - 2 * (q % 2), (q + 2) % PLANE
    up, down = r + PLANE, r - PLANE
    has_up, has_down = line < lines - 1, line > 0
    core = (r, 1 - c)

    def rows_of(t, who):
        return pl.ds(pl.multiple_of((t * PLANE + who) * quarter, quarter), quarter)

    own = emb_ref.at[pl.ds(pl.multiple_of(c * quarter, quarter), quarter)]

    def remote(src, dst, kind, t, dev):
        return pltpu.make_async_remote_copy(
            src_ref=src, dst_ref=dst, send_sem=send.at[kind, t], recv_sem=recv.at[kind, t],
            device_id=dev, device_id_type=MESH,
        )

    def whole(kind, t, who, dev, first=False):
        dst = col_ref.at[rows_of(t, who)]
        return remote(own if first else dst, dst, kind, t, dev)

    def part(kind, t, who, side, dev):
        dst = col_ref.at[rows_of(t, who), pl.ds(side * half, half)]
        return remote(dst, dst, kind, t, dev)

    barrier = pltpu.get_barrier_semaphore()
    for dev in ((x, c), (y, c), core):
        pl.semaphore_signal(barrier, inc=1, device_id=dev, device_id_type=MESH)

    @pl.when(has_up)
    def _():
        pl.semaphore_signal(barrier, inc=1, device_id=(up, c), device_id_type=MESH)

    @pl.when(has_down)
    def _():
        pl.semaphore_signal(barrier, inc=1, device_id=(down, c), device_id_type=MESH)

    pl.semaphore_wait(barrier, 3 + jnp.where(has_up, 1, 0) + jnp.where(has_down, 1, 0))

    def send_on(t, first=False):
        whole(2, t, q, (x, c), first).start()
        whole(3, t, q, (y, c), first).start()

    own_copy = pltpu.make_async_copy(own, col_ref.at[rows_of(line, q)], send.at[7, 0])
    tgt_copy = pltpu.make_async_copy(tgt_ref, all_tgt_ref.at[c], send.at[7, 1])

    @pl.when(has_up)
    def _():
        whole(0, line, q, (up, c), True).start()

    @pl.when(has_down)
    def _():
        whole(1, line, q, (down, c), True).start()

    send_on(line, True)
    own_copy.start()
    tgt_copy.start()
    tgt_swap = remote(tgt_ref, all_tgt_ref.at[c], 6, 0, core)
    tgt_swap.start()

    def ring_stage(t):
        whole(2, t, qx, (x, c)).wait_recv()
        part(5, t, qx, 0, (y, c)).start()
        whole(3, t, qy, (y, c)).wait_recv()
        part(4, t, qy, 1, (x, c)).start()

    for step in range(1, lines + 1):
        if step < lines:
            @pl.when(line - step >= 0)
            def _(step=step):
                t = line - step
                whole(0, t, q, (up, c)).wait_recv()

                @pl.when(has_up)
                def _():
                    whole(0, t, q, (up, c)).start()

                send_on(t)

            @pl.when(line + step < lines)
            def _(step=step):
                t = line + step
                whole(1, t, q, (down, c)).wait_recv()

                @pl.when(has_down)
                def _():
                    whole(1, t, q, (down, c)).start()

                send_on(t)

        if step == 1:
            ring_stage(line)
        else:
            @pl.when(line - (step - 1) >= 0)
            def _(step=step):
                ring_stage(line - (step - 1))

            @pl.when(line + (step - 1) < lines)
            def _(step=step):
                ring_stage(line + (step - 1))

    opposite = (q + 2 - 4 * (q // 2)) + 1 - 2 * (q % 2)
    for t in range(lines):
        part(4, t, opposite, 1, (x, c)).wait_recv()
        part(5, t, opposite, 0, (y, c)).wait_recv()
    own_copy.wait()

    heads = col_ref.at[pl.ds(0, PW)]
    head_copy = pltpu.make_async_copy(heads, head_ref.at[c], send.at[7, 2])
    head_swap = remote(heads, head_ref.at[c], 6, 1, core)
    head_copy.start()
    head_swap.start()

    for t in range(lines):
        whole(2, t, q, (x, c)).wait_send()
        whole(3, t, q, (y, c)).wait_send()
        part(4, t, qy, 1, (x, c)).wait_send()
        part(5, t, qx, 0, (y, c)).wait_send()

        @pl.when(has_up & (t <= line))
        def _(t=t):
            whole(0, t, q, (up, c)).wait_send()

        @pl.when(has_down & (t >= line))
        def _(t=t):
            whole(1, t, q, (down, c)).wait_send()

    tgt_copy.wait()
    head_copy.wait()
    remote(tgt_ref, all_tgt_ref.at[1 - c], 6, 0, core).wait()
    remote(heads, head_ref.at[1 - c], 6, 1, core).wait()


def gather(embedded, targets, n_rows):
    width = embedded.shape[1]
    return pl.pallas_call(
        gather_kernel,
        out_shape=(
            jax.ShapeDtypeStruct((C // 2, width), jnp.float32),
            jax.ShapeDtypeStruct((2, PW, width), jnp.float32),
            jax.ShapeDtypeStruct((2,) + targets.shape, jnp.float32),
        ),
        in_specs=[pl.BlockSpec(memory_space=pl.ANY)] * 2,
        out_specs=(pl.BlockSpec(memory_space=pl.ANY),) * 3,
        scratch_shapes=[
            pltpu.SemaphoreType.DMA((8, max(n_rows // PLANE, 3))),
            pltpu.SemaphoreType.DMA((8, max(n_rows // PLANE, 3))),
        ],
        compiler_params=pltpu.CompilerParams(collective_id=0, has_side_effects=True),
    )(embedded, targets)


def head_gaussian(left_rows, heads, heads_sq):
    left_sq = jnp.sum(left_rows * left_rows, axis=1, keepdims=True)
    return jnp.exp(
        -(left_sq + heads_sq - 2.0 * dot_t(left_rows, heads)) / (2.0 * left_rows.shape[1])
    )


def iota(shape, axis):
    return lax.broadcasted_iota(jnp.int32, shape, axis)


def eliminate(work, first, size):
    n = work.shape[0]
    start = pl.multiple_of(first * size, size)
    rows = work[pl.ds(start, size), :]
    rolled = pltpu.roll(rows, n - start, 1)
    lane = iota((size, 128), 1)
    row = iota((size, 128), 0)
    pair = jnp.where(lane < size, rolled[:, :128], jnp.where(lane == row + size, 1.0, 0.0))
    for j in range(size - 1):
        column = pair[:, j : j + 1]
        scaled = pair[j : j + 1, :] / pair[j : j + 1, j : j + 1]
        pair = pair - jnp.where(row > j, column, 0.0) * scaled
    diagonal = jnp.sum(jnp.where(lane == row, pair, 0.0), axis=1, keepdims=True)
    block_inv = (pair / jnp.sqrt(diagonal))[:, size : 2 * size]

    wide_lane = iota((size, n), 1) - start
    inside = (wide_lane >= 0) & (wide_lane < size)
    eye = jnp.where(wide_lane == iota((size, n), 0), 1.0, 0.0)
    done = jnp.dot(
        block_inv, jnp.where(inside, eye, rows), precision=exact_mode, preferred_element_type=jnp.float32
    )
    below = jnp.where(wide_lane >= size, done, 0.0)
    update = lax.dot_general(
        below, done, (((0,), (0,)), ((), ())), precision=exact_mode, preferred_element_type=jnp.float32
    )
    all_row = iota((n, n), 0) - start
    all_lane = iota((n, n), 1) - start
    keep = jnp.where((all_row >= size) & (all_lane >= 0) & (all_lane < size), 0.0, work[...])
    work[...] = keep - update
    work[pl.ds(start, size), :] = done


def finish_kernel(
    ridge_ref, part_ref, emb_ref, col_ref, head_ref, slab_ref, out_ref, panel_ref, rem_ref,
    opp_x, opp_y, from_x, from_y, to_x, to_y, acc, from_down, from_up, work, land, head_slab, send, recv,
):
    r = lax.axis_index("rows")
    c = lax.axis_index("cols")
    n_rows = lax.axis_size("rows")
    lines = n_rows // PLANE
    line, q = r // PLANE, r % PLANE
    qx, qy = q + 1 - 2 * (q % 2), (q + 2) % PLANE
    opposite = PLANE - 1 - q
    x, y = (line * PLANE + qx, c), (line * PLANE + qy, c)
    up, down = (r + PLANE, c), (r - PLANE, c)
    has_up, has_down = line < lines - 1, line > 0
    wide = part_ref.shape[2]
    half = wide // 2
    lo, hi = pl.ds(0, half), pl.ds(half, half)
    rows_here = emb_ref.shape[0]
    half_cols = col_ref.shape[0]
    quarter = half_cols // n_rows
    n_head = head_ref.shape[0]
    pw = n_head // 2
    ridge = ridge_ref[0]

    def remote(src, dst, kind, t, dev):
        return pltpu.make_async_remote_copy(
            src_ref=src, dst_ref=dst, send_sem=send.at[kind, t], recv_sem=recv.at[kind, t],
            device_id=dev, device_id_type=MESH,
        )

    def c_opp_x(t):
        return remote(part_ref.at[t * PLANE + opposite, :, lo], opp_x.at[t], 0, t, x)

    def c_opp_y(t):
        return remote(part_ref.at[t * PLANE + opposite, :, hi], opp_y.at[t], 1, t, y)

    def c_plain_x(t):
        return remote(part_ref.at[t * PLANE + qx, :, lo], from_x.at[t, :, lo], 2, t, x)

    def c_plain_y(t):
        return remote(part_ref.at[t * PLANE + qy, :, hi], from_y.at[t, :, hi], 3, t, y)

    def c_sum_x(t):
        return remote(to_x.at[t], from_x.at[t, :, hi], 4, t, x)

    def c_sum_y(t):
        return remote(to_y.at[t], from_y.at[t, :, lo], 5, t, y)

    def c_up(t):
        return remote(acc.at[t], from_down.at[t], 6, t, up)

    def c_down(t):
        return remote(acc.at[t], from_up.at[t], 7, t, down)

    barrier = pltpu.get_barrier_semaphore()
    for dev in (x, y):
        pl.semaphore_signal(barrier, inc=1, device_id=dev, device_id_type=MESH)

    @pl.when(has_up)
    def _():
        pl.semaphore_signal(barrier, inc=1, device_id=up, device_id_type=MESH)

    @pl.when(has_down)
    def _():
        pl.semaphore_signal(barrier, inc=1, device_id=down, device_id_type=MESH)

    pl.semaphore_wait(barrier, 2 + jnp.where(has_up, 1, 0) + jnp.where(has_down, 1, 0))

    order = []
    for t in range((lines + 1) // 2):
        order += [t] if t == lines - 1 - t else [t, lines - 1 - t]
    for t in order:
        c_opp_x(t).start()
        c_opp_y(t).start()
    for t in order:
        c_plain_x(t).start()
        c_plain_y(t).start()

    heads = head_ref[...]
    heads_sq = dot_t(jnp.ones((8, heads.shape[1]), jnp.float32), heads * heads)[:1]
    same = iota((n_head, n_head), 0) == iota((n_head, n_head), 1)
    work[...] = head_gaussian(heads, heads, heads_sq) + jnp.where(same, ridge, 0.0)

    def ring_sum(t):
        c_opp_x(t).wait_recv()
        to_y[t] = part_ref[t * PLANE + qy, :, lo] + opp_x[t]
        c_sum_y(t).start()
        c_opp_y(t).wait_recv()
        to_x[t] = part_ref[t * PLANE + qx, :, hi] + opp_y[t]
        c_sum_x(t).start()

    def line_sum(t):
        c_plain_x(t).wait_recv()
        c_plain_y(t).wait_recv()
        c_sum_x(t).wait_recv()
        c_sum_y(t).wait_recv()
        acc[t] = part_ref[t * PLANE + q] + from_x[t] + from_y[t]

        @pl.when(has_down & (t >= line))
        def _():
            c_up(t).wait_recv()
            acc[t] = acc[t] + from_down[t]

        @pl.when(has_up & (t <= line))
        def _():
            c_down(t).wait_recv()
            acc[t] = acc[t] + from_up[t]

        @pl.when(t > line)
        def _():
            c_up(t).start()

        @pl.when(t < line)
        def _():
            c_down(t).start()

        @pl.when(t == line)
        def _():
            out_ref[...] = acc[t]

    blocks = n_head // BLOCK

    def some_blocks(a, b):
        lax.fori_loop(a, b, lambda i, _: (eliminate(work, i, BLOCK), 0)[1], 0)

    cuts = [blocks * i // (len(order) + 1) for i in range(len(order) + 2)]
    some_blocks(cuts[0], cuts[1])
    for t in order:
        ring_sum(t)
    for i, t in enumerate(order):
        some_blocks(cuts[i + 1], cuts[i + 2])
        line_sum(t)

    head_row = iota((rows_here, n_head), 0)
    head_col = iota((rows_here, n_head), 1)
    block = head_col // pw
    offset = head_row - block * quarter
    hits = (offset >= 0) & (offset < quarter) & (head_col - block * pw == r * quarter + offset)
    head_slab[...] = head_gaussian(emb_ref[...], heads, heads_sq) + jnp.where(hits, ridge, 0.0)

    chunk = n_head

    def land_chunk(i, _):
        start = pl.multiple_of(i * chunk, chunk)
        row = iota((chunk, n_head), 0) + start
        hit = (row < pw) & (iota((chunk, n_head), 1) == c * pw + row)
        land[pl.ds(start, chunk), :] = head_gaussian(
            col_ref[pl.ds(start, chunk), :], heads, heads_sq
        ) + jnp.where(hit, ridge, 0.0)
        return 0

    lax.fori_loop(0, half_cols // chunk, land_chunk, 0)

    lower = iota((n_head, n_head), 1) // BLOCK <= iota((n_head, n_head), 0) // BLOCK
    inverse = jnp.where(lower, work[...], 0.0)
    panels = dot_t(head_slab[...], inverse)
    panel_ref[...] = panels
    for first in range(pw, half_cols, pw):
        rows = dot_t(land[first : first + pw, :], inverse)
        rem_ref[:, first - pw : first] = slab_ref[:, first : first + pw] - dot_t(panels, rows)

    for t in range(lines):
        for copy in (c_opp_x, c_opp_y, c_plain_x, c_plain_y, c_sum_x, c_sum_y):
            copy(t).wait_send()

        @pl.when(t > line)
        def _(t=t):
            c_up(t).wait_send()

        @pl.when(t < line)
        def _(t=t):
            c_down(t).wait_send()


def finish(ridge_shift, partial, embedded, column_emb, heads, kernel_slab, n_rows):
    lines = n_rows // PLANE
    _, share, wide = partial.shape
    n_head = heads.shape[0]
    rows_here = embedded.shape[0]
    vmem = pl.BlockSpec(memory_space=pltpu.VMEM)
    full = pltpu.VMEM((lines, share, wide), jnp.float32)
    halved = pltpu.VMEM((lines, share, wide // 2), jnp.float32)
    return pl.pallas_call(
        finish_kernel,
        out_shape=(
            jax.ShapeDtypeStruct((share, wide), jnp.float32),
            jax.ShapeDtypeStruct((rows_here, n_head), jnp.float32),
            jax.ShapeDtypeStruct((rows_here, wide - PW), jnp.float32),
        ),
        in_specs=[pl.BlockSpec(memory_space=pltpu.SMEM)] + [vmem] * 5,
        out_specs=(vmem,) * 3,
        scratch_shapes=[
            halved, halved, full, full, halved, halved, full, full, full,
            pltpu.VMEM((n_head, n_head), jnp.float32),
            pltpu.VMEM((wide, n_head), jnp.float32),
            pltpu.VMEM((rows_here, n_head), jnp.float32),
            pltpu.SemaphoreType.DMA((8, lines)),
            pltpu.SemaphoreType.DMA((8, lines)),
        ],
        compiler_params=pltpu.CompilerParams(
            collective_id=1, has_side_effects=True, vmem_limit_bytes=48 * 1024 * 1024
        ),
    )(ridge_shift, partial, embedded, column_emb, heads, kernel_slab)


def per_device(points, landmark_index, targets, ridge_shift):
    rows_here = landmark_index.shape[0]
    block_points = points.shape[0]
    row_pos = lax.axis_index("rows")
    col_pos = lax.axis_index("cols")
    n_rows = lax.axis_size("rows")
    half_cols = C // 2
    quarter = half_cols // n_rows
    ridge = ridge_shift[0]
    local_index = landmark_index - row_pos * block_points
    embedded = jnp.take(points, local_index, axis=0)
    column_emb, head_pair, target_pair = gather(embedded, targets, n_rows)
    heads = head_pair.reshape(2 * PW, -1)
    all_targets = jnp.concatenate([target_pair[0], target_pair[1]], axis=1)

    row_ids = lax.broadcasted_iota(jnp.int32, (rows_here, half_cols), 0)
    col_ids = lax.broadcasted_iota(jnp.int32, (rows_here, half_cols), 1)
    offset = row_ids - col_pos * quarter
    ridge_hits = (offset >= 0) & (offset < quarter) & (col_ids == row_pos * quarter + offset)
    kernel_slab = gaussian(embedded, column_emb) + jnp.where(ridge_hits, ridge, 0.0)
    partial = lax.dot_general(
        all_targets,
        kernel_slab,
        (((0,), (0,)), ((), ())),
        precision=exact_mode,
        preferred_element_type=jnp.float32,
    )
    share = partial.shape[0] // n_rows
    return finish(
        ridge_shift, partial.reshape(n_rows, share, half_cols), embedded, column_emb, heads, kernel_slab, n_rows
    )


def solution(mesh):
    in_specs = (P("rows", None), P("rows"), P("rows", "cols"), P())
    out_specs = (P("rows", "cols"), P("rows", None), P("rows", "cols"))
    return jax.shard_map(
        per_device, mesh=mesh, in_specs=in_specs, out_specs=out_specs, check_vma=False
    )
```

```python
import jax
import jax.numpy as jnp
from jax import lax
from jax.experimental import pallas as pl
from jax.experimental.pallas import tpu as pltpu
from jax.sharding import PartitionSpec as P

C = 2048
PW = 128
BLOCK = 32

exact_mode = lax.Precision.HIGHEST


def dot_t(left, right):
    return lax.dot_general(
        left, right, (((1,), (1,)), ((), ())), precision=exact_mode, preferred_element_type=jnp.float32
    )


def gaussian(left_rows, right_rows):
    left_sq = jnp.sum(left_rows * left_rows, axis=1)
    right_sq = jnp.sum(right_rows * right_rows, axis=1)
    cross_term = dot_t(left_rows, right_rows)
    return jnp.exp(
        -(left_sq[:, None] + right_sq[None, :] - 2.0 * cross_term) / (2.0 * left_rows.shape[1])
    )


MESH = pl.DeviceIdType.MESH
PLANE = 4


def gather_kernel(emb_ref, tgt_ref, col_ref, head_ref, all_tgt_ref, send, recv):
    r = lax.axis_index("rows")
    c = lax.axis_index("cols")
    n_rows = lax.axis_size("rows")
    lines = n_rows // PLANE
    line, q = r // PLANE, r % PLANE
    quarter = col_ref.shape[0] // n_rows
    half = col_ref.shape[1] // 2
    x = line * PLANE + (q + 1 - 2 * (q % 2))
    y = line * PLANE + (q + 2) % PLANE
    qx, qy = q + 1 - 2 * (q % 2), (q + 2) % PLANE
    up, down = r + PLANE, r - PLANE
    has_up, has_down = line < lines - 1, line > 0
    core = (r, 1 - c)

    def rows_of(t, who):
        return pl.ds(pl.multiple_of((t * PLANE + who) * quarter, quarter), quarter)

    own = emb_ref.at[pl.ds(pl.multiple_of(c * quarter, quarter), quarter)]

    def remote(src, dst, kind, t, dev):
        return pltpu.make_async_remote_copy(
            src_ref=src, dst_ref=dst, send_sem=send.at[kind, t], recv_sem=recv.at[kind, t],
            device_id=dev, device_id_type=MESH,
        )

    def whole(kind, t, who, dev, first=False):
        dst = col_ref.at[rows_of(t, who)]
        return remote(own if first else dst, dst, kind, t, dev)

    def part(kind, t, who, side, dev):
        dst = col_ref.at[rows_of(t, who), pl.ds(side * half, half)]
        return remote(dst, dst, kind, t, dev)

    barrier = pltpu.get_barrier_semaphore()
    for dev in ((x, c), (y, c), core):
        pl.semaphore_signal(barrier, inc=1, device_id=dev, device_id_type=MESH)

    @pl.when(has_up)
    def _():
        pl.semaphore_signal(barrier, inc=1, device_id=(up, c), device_id_type=MESH)

    @pl.when(has_down)
    def _():
        pl.semaphore_signal(barrier, inc=1, device_id=(down, c), device_id_type=MESH)

    pl.semaphore_wait(barrier, 3 + jnp.where(has_up, 1, 0) + jnp.where(has_down, 1, 0))

    def send_on(t, first=False):
        whole(2, t, q, (x, c), first).start()
        whole(3, t, q, (y, c), first).start()

    own_copy = pltpu.make_async_copy(own, col_ref.at[rows_of(line, q)], send.at[7, 0])
    tgt_copy = pltpu.make_async_copy(tgt_ref, all_tgt_ref.at[c], send.at[7, 1])

    @pl.when(has_up)
    def _():
        whole(0, line, q, (up, c), True).start()

    @pl.when(has_down)
    def _():
        whole(1, line, q, (down, c), True).start()

    send_on(line, True)
    own_copy.start()
    tgt_copy.start()
    tgt_swap = remote(tgt_ref, all_tgt_ref.at[c], 6, 0, core)
    tgt_swap.start()

    def ring_stage(t):
        whole(2, t, qx, (x, c)).wait_recv()
        part(5, t, qx, 0, (y, c)).start()
        whole(3, t, qy, (y, c)).wait_recv()
        part(4, t, qy, 1, (x, c)).start()

    for step in range(1, lines + 1):
        if step < lines:
            @pl.when(line - step >= 0)
            def _(step=step):
                t = line - step
                whole(0, t, q, (up, c)).wait_recv()

                @pl.when(has_up)
                def _():
                    whole(0, t, q, (up, c)).start()

                send_on(t)

            @pl.when(line + step < lines)
            def _(step=step):
                t = line + step
                whole(1, t, q, (down, c)).wait_recv()

                @pl.when(has_down)
                def _():
                    whole(1, t, q, (down, c)).start()

                send_on(t)

        if step == 1:
            ring_stage(line)
        else:
            @pl.when(line - (step - 1) >= 0)
            def _(step=step):
                ring_stage(line - (step - 1))

            @pl.when(line + (step - 1) < lines)
            def _(step=step):
                ring_stage(line + (step - 1))

    opposite = (q + 2 - 4 * (q // 2)) + 1 - 2 * (q % 2)
    for t in range(lines):
        part(4, t, opposite, 1, (x, c)).wait_recv()
        part(5, t, opposite, 0, (y, c)).wait_recv()
    own_copy.wait()

    heads = col_ref.at[pl.ds(0, PW)]
    head_copy = pltpu.make_async_copy(heads, head_ref.at[c], send.at[7, 2])
    head_swap = remote(heads, head_ref.at[c], 6, 1, core)
    head_copy.start()
    head_swap.start()

    for t in range(lines):
        whole(2, t, q, (x, c)).wait_send()
        whole(3, t, q, (y, c)).wait_send()
        part(4, t, qy, 1, (x, c)).wait_send()
        part(5, t, qx, 0, (y, c)).wait_send()

        @pl.when(has_up & (t <= line))
        def _(t=t):
            whole(0, t, q, (up, c)).wait_send()

        @pl.when(has_down & (t >= line))
        def _(t=t):
            whole(1, t, q, (down, c)).wait_send()

    tgt_copy.wait()
    head_copy.wait()
    remote(tgt_ref, all_tgt_ref.at[1 - c], 6, 0, core).wait()
    remote(heads, head_ref.at[1 - c], 6, 1, core).wait()


def gather(embedded, targets, n_rows):
    width = embedded.shape[1]
    return pl.pallas_call(
        gather_kernel,
        out_shape=(
            jax.ShapeDtypeStruct((C // 2, width), jnp.float32),
            jax.ShapeDtypeStruct((2, PW, width), jnp.float32),
            jax.ShapeDtypeStruct((2,) + targets.shape, jnp.float32),
        ),
        in_specs=[pl.BlockSpec(memory_space=pl.ANY)] * 2,
        out_specs=(pl.BlockSpec(memory_space=pl.ANY),) * 3,
        scratch_shapes=[
            pltpu.SemaphoreType.DMA((8, max(n_rows // PLANE, 3))),
            pltpu.SemaphoreType.DMA((8, max(n_rows // PLANE, 3))),
        ],
        compiler_params=pltpu.CompilerParams(collective_id=0, has_side_effects=True),
    )(embedded, targets)


def head_gaussian(left_rows, heads, heads_sq):
    left_sq = jnp.sum(left_rows * left_rows, axis=1, keepdims=True)
    return jnp.exp(
        -(left_sq + heads_sq - 2.0 * dot_t(left_rows, heads)) / (2.0 * left_rows.shape[1])
    )


def iota(shape, axis):
    return lax.broadcasted_iota(jnp.int32, shape, axis)


def eliminate(work, first, size):
    n = work.shape[0]
    start = pl.multiple_of(first * size, size)
    rows = work[pl.ds(start, size), :]
    rolled = pltpu.roll(rows, n - start, 1)
    lane = iota((size, 128), 1)
    row = iota((size, 128), 0)
    pair = jnp.where(lane < size, rolled[:, :128], jnp.where(lane == row + size, 1.0, 0.0))
    for j in range(size - 1):
        column = pair[:, j : j + 1]
        scaled = pair[j : j + 1, :] / pair[j : j + 1, j : j + 1]
        pair = pair - jnp.where(row > j, column, 0.0) * scaled
    diagonal = jnp.sum(jnp.where(lane == row, pair, 0.0), axis=1, keepdims=True)
    block_inv = (pair / jnp.sqrt(diagonal))[:, size : 2 * size]

    wide_lane = iota((size, n), 1) - start
    inside = (wide_lane >= 0) & (wide_lane < size)
    eye = jnp.where(wide_lane == iota((size, n), 0), 1.0, 0.0)
    done = jnp.dot(
        block_inv, jnp.where(inside, eye, rows), precision=exact_mode, preferred_element_type=jnp.float32
    )
    below = jnp.where(wide_lane >= size, done, 0.0)
    update = lax.dot_general(
        below, done, (((0,), (0,)), ((), ())), precision=exact_mode, preferred_element_type=jnp.float32
    )
    all_row = iota((n, n), 0) - start
    all_lane = iota((n, n), 1) - start
    keep = jnp.where((all_row >= size) & (all_lane >= 0) & (all_lane < size), 0.0, work[...])
    work[...] = keep - update
    work[pl.ds(start, size), :] = done


def finish_kernel(
    ridge_ref, part_ref, emb_ref, col_ref, head_ref, slab_ref, out_ref, panel_ref, rem_ref,
    opp_x, opp_y, from_x, from_y, to_x, to_y, acc, from_down, from_up, work, land, head_slab, send, recv,
):
    r = lax.axis_index("rows")
    c = lax.axis_index("cols")
    n_rows = lax.axis_size("rows")
    lines = n_rows // PLANE
    line, q = r // PLANE, r % PLANE
    qx, qy = q + 1 - 2 * (q % 2), (q + 2) % PLANE
    opposite = PLANE - 1 - q
    x, y = (line * PLANE + qx, c), (line * PLANE + qy, c)
    up, down = (r + PLANE, c), (r - PLANE, c)
    has_up, has_down = line < lines - 1, line > 0
    wide = part_ref.shape[2]
    half = wide // 2
    lo, hi = pl.ds(0, half), pl.ds(half, half)
    rows_here = emb_ref.shape[0]
    half_cols = col_ref.shape[0]
    quarter = half_cols // n_rows
    n_head = head_ref.shape[0]
    pw = n_head // 2
    ridge = ridge_ref[0]

    def remote(src, dst, kind, t, dev):
        return pltpu.make_async_remote_copy(
            src_ref=src, dst_ref=dst, send_sem=send.at[kind, t], recv_sem=recv.at[kind, t],
            device_id=dev, device_id_type=MESH,
        )

    def c_opp_x(t):
        return remote(part_ref.at[t * PLANE + opposite, :, lo], opp_x.at[t], 0, t, x)

    def c_opp_y(t):
        return remote(part_ref.at[t * PLANE + opposite, :, hi], opp_y.at[t], 1, t, y)

    def c_plain_x(t):
        return remote(part_ref.at[t * PLANE + qx, :, lo], from_x.at[t, :, lo], 2, t, x)

    def c_plain_y(t):
        return remote(part_ref.at[t * PLANE + qy, :, hi], from_y.at[t, :, hi], 3, t, y)

    def c_sum_x(t):
        return remote(to_x.at[t], from_x.at[t, :, hi], 4, t, x)

    def c_sum_y(t):
        return remote(to_y.at[t], from_y.at[t, :, lo], 5, t, y)

    def c_up(t):
        return remote(acc.at[t], from_down.at[t], 6, t, up)

    def c_down(t):
        return remote(acc.at[t], from_up.at[t], 7, t, down)

    barrier = pltpu.get_barrier_semaphore()
    for dev in (x, y):
        pl.semaphore_signal(barrier, inc=1, device_id=dev, device_id_type=MESH)

    @pl.when(has_up)
    def _():
        pl.semaphore_signal(barrier, inc=1, device_id=up, device_id_type=MESH)

    @pl.when(has_down)
    def _():
        pl.semaphore_signal(barrier, inc=1, device_id=down, device_id_type=MESH)

    pl.semaphore_wait(barrier, 2 + jnp.where(has_up, 1, 0) + jnp.where(has_down, 1, 0))

    order = []
    for t in range((lines + 1) // 2):
        order += [t] if t == lines - 1 - t else [t, lines - 1 - t]
    for t in order:
        c_opp_x(t).start()
        c_opp_y(t).start()
    for t in order:
        c_plain_x(t).start()
        c_plain_y(t).start()

    heads = head_ref[...]
    heads_sq = dot_t(jnp.ones((8, heads.shape[1]), jnp.float32), heads * heads)[:1]
    same = iota((n_head, n_head), 0) == iota((n_head, n_head), 1)
    work[...] = head_gaussian(heads, heads, heads_sq) + jnp.where(same, ridge, 0.0)

    def ring_sum(t):
        c_opp_x(t).wait_recv()
        to_y[t] = part_ref[t * PLANE + qy, :, lo] + opp_x[t]
        c_sum_y(t).start()
        c_opp_y(t).wait_recv()
        to_x[t] = part_ref[t * PLANE + qx, :, hi] + opp_y[t]
        c_sum_x(t).start()

    def ring_total(t):
        c_plain_x(t).wait_recv()
        c_plain_y(t).wait_recv()
        c_sum_x(t).wait_recv()
        c_sum_y(t).wait_recv()
        acc[t] = part_ref[t * PLANE + q] + from_x[t] + from_y[t]

    def line_step(step):
        @pl.when(line <= step)
        def _():
            t = lines - 1 - step + line

            @pl.when(has_down)
            def _():
                c_up(t).wait_recv()
                acc[t] = acc[t] + from_down[t]

            c_up(t).start()

        @pl.when(lines - 1 - line <= step)
        def _():
            t = step - (lines - 1 - line)

            @pl.when(has_up)
            def _():
                c_down(t).wait_recv()
                acc[t] = acc[t] + from_up[t]

            c_down(t).start()

    def line_end():
        out_ref[...] = acc[line]

        @pl.when(has_down)
        def _():
            c_up(line).wait_recv()
            out_ref[...] += from_down[line]

        @pl.when(has_up)
        def _():
            c_down(line).wait_recv()
            out_ref[...] += from_up[line]

    blocks = n_head // BLOCK

    def some_blocks(a, b):
        lax.fori_loop(a, b, lambda i, _: (eliminate(work, i, BLOCK), 0)[1], 0)

    head_row = iota((rows_here, n_head), 0)
    head_col = iota((rows_here, n_head), 1)
    block = head_col // pw
    offset = head_row - block * quarter
    hits = (offset >= 0) & (offset < quarter) & (head_col - block * pw == r * quarter + offset)
    head_slab[...] = head_gaussian(emb_ref[...], heads, heads_sq) + jnp.where(hits, ridge, 0.0)

    chunk = n_head

    def land_chunk(i, _):
        start = pl.multiple_of(i * chunk, chunk)
        row = iota((chunk, n_head), 0) + start
        hit = (row < pw) & (iota((chunk, n_head), 1) == c * pw + row)
        land[pl.ds(start, chunk), :] = head_gaussian(
            col_ref[pl.ds(start, chunk), :], heads, heads_sq
        ) + jnp.where(hit, ridge, 0.0)
        return 0

    lax.fori_loop(0, half_cols // chunk, land_chunk, 0)

    some_blocks(0, blocks // 8)
    for t in order:
        ring_sum(t)
    some_blocks(blocks // 8, blocks * 3 // 8)
    ring_total(order[0])
    if lines > 1:
        ring_total(order[1])
    if lines > 1:
        line_step(0)
    some_blocks(blocks * 3 // 8, blocks // 2)
    for t in order[2:]:
        ring_total(t)
    if lines > 2:
        line_step(1)
    some_blocks(blocks // 2, blocks * 5 // 8)
    if lines > 3:
        line_step(2)
    some_blocks(blocks * 5 // 8, blocks)
    for step in range(3, lines - 1):
        line_step(step)

    lower = iota((n_head, n_head), 1) // BLOCK <= iota((n_head, n_head), 0) // BLOCK
    inverse = jnp.where(lower, work[...], 0.0)
    panels = dot_t(head_slab[...], inverse)
    panel_ref[...] = panels
    for first in range(pw, half_cols, pw):
        rows = dot_t(land[first : first + pw, :], inverse)
        rem_ref[:, first - pw : first] = slab_ref[:, first : first + pw] - dot_t(panels, rows)

    line_end()
    for t in range(lines):
        for copy in (c_opp_x, c_opp_y, c_plain_x, c_plain_y, c_sum_x, c_sum_y):
            copy(t).wait_send()

        @pl.when(t > line)
        def _(t=t):
            c_up(t).wait_send()

        @pl.when(t < line)
        def _(t=t):
            c_down(t).wait_send()


def finish(ridge_shift, partial, embedded, column_emb, heads, kernel_slab, n_rows):
    lines = n_rows // PLANE
    _, share, wide = partial.shape
    n_head = heads.shape[0]
    rows_here = embedded.shape[0]
    vmem = pl.BlockSpec(memory_space=pltpu.VMEM)
    full = pltpu.VMEM((lines, share, wide), jnp.float32)
    halved = pltpu.VMEM((lines, share, wide // 2), jnp.float32)
    return pl.pallas_call(
        finish_kernel,
        out_shape=(
            jax.ShapeDtypeStruct((share, wide), jnp.float32),
            jax.ShapeDtypeStruct((rows_here, n_head), jnp.float32),
            jax.ShapeDtypeStruct((rows_here, wide - PW), jnp.float32),
        ),
        in_specs=[pl.BlockSpec(memory_space=pltpu.SMEM)] + [vmem] * 5,
        out_specs=(vmem,) * 3,
        scratch_shapes=[
            halved, halved, full, full, halved, halved, full, full, full,
            pltpu.VMEM((n_head, n_head), jnp.float32),
            pltpu.VMEM((wide, n_head), jnp.float32),
            pltpu.VMEM((rows_here, n_head), jnp.float32),
            pltpu.SemaphoreType.DMA((8, lines)),
            pltpu.SemaphoreType.DMA((8, lines)),
        ],
        compiler_params=pltpu.CompilerParams(
            collective_id=1, has_side_effects=True, vmem_limit_bytes=48 * 1024 * 1024
        ),
    )(ridge_shift, partial, embedded, column_emb, heads, kernel_slab)


def per_device(points, landmark_index, targets, ridge_shift):
    rows_here = landmark_index.shape[0]
    block_points = points.shape[0]
    row_pos = lax.axis_index("rows")
    col_pos = lax.axis_index("cols")
    n_rows = lax.axis_size("rows")
    half_cols = C // 2
    quarter = half_cols // n_rows
    ridge = ridge_shift[0]
    local_index = landmark_index - row_pos * block_points
    embedded = jnp.take(points, local_index, axis=0)
    column_emb, head_pair, target_pair = gather(embedded, targets, n_rows)
    heads = head_pair.reshape(2 * PW, -1)
    all_targets = jnp.concatenate([target_pair[0], target_pair[1]], axis=1)

    row_ids = lax.broadcasted_iota(jnp.int32, (rows_here, half_cols), 0)
    col_ids = lax.broadcasted_iota(jnp.int32, (rows_here, half_cols), 1)
    offset = row_ids - col_pos * quarter
    ridge_hits = (offset >= 0) & (offset < quarter) & (col_ids == row_pos * quarter + offset)
    kernel_slab = gaussian(embedded, column_emb) + jnp.where(ridge_hits, ridge, 0.0)
    partial = lax.dot_general(
        all_targets,
        kernel_slab,
        (((0,), (0,)), ((), ())),
        precision=exact_mode,
        preferred_element_type=jnp.float32,
    )
    share = partial.shape[0] // n_rows
    return finish(
        ridge_shift, partial.reshape(n_rows, share, half_cols), embedded, column_emb, heads, kernel_slab, n_rows
    )


def solution(mesh):
    in_specs = (P("rows", None), P("rows"), P("rows", "cols"), P())
    out_specs = (P("rows", "cols"), P("rows", None), P("rows", "cols"))
    return jax.shard_map(
        per_device, mesh=mesh, in_specs=in_specs, out_specs=out_specs, check_vma=False
    )
```

```python
import jax
import jax.numpy as jnp
from jax import lax
from jax.experimental import pallas as pl
from jax.experimental.pallas import tpu as pltpu
from jax.sharding import PartitionSpec as P

C = 2048
PW = 128
BLOCK = 32

exact_mode = lax.Precision.HIGHEST


def dot_t(left, right):
    return lax.dot_general(
        left, right, (((1,), (1,)), ((), ())), precision=exact_mode, preferred_element_type=jnp.float32
    )


def gaussian(left_rows, right_rows):
    left_sq = jnp.sum(left_rows * left_rows, axis=1)
    right_sq = jnp.sum(right_rows * right_rows, axis=1)
    cross_term = dot_t(left_rows, right_rows)
    return jnp.exp(
        -(left_sq[:, None] + right_sq[None, :] - 2.0 * cross_term) / (2.0 * left_rows.shape[1])
    )


MESH = pl.DeviceIdType.MESH
PLANE = 4


def head_gaussian(left_rows, heads, heads_sq):
    left_sq = jnp.sum(left_rows * left_rows, axis=1, keepdims=True)
    return jnp.exp(
        -(left_sq + heads_sq - 2.0 * dot_t(left_rows, heads)) / (2.0 * left_rows.shape[1])
    )


def iota(shape, axis):
    return lax.broadcasted_iota(jnp.int32, shape, axis)


def eliminate(work, first, size):
    n = work.shape[0]
    start = pl.multiple_of(first * size, size)
    rows = work[pl.ds(start, size), :]
    rolled = pltpu.roll(rows, n - start, 1)
    lane = iota((size, 128), 1)
    row = iota((size, 128), 0)
    pair = jnp.where(lane < size, rolled[:, :128], jnp.where(lane == row + size, 1.0, 0.0))
    for j in range(0, size, 2):
        k = j + 1
        first_row, second_row = pair[j:k, :], pair[k : k + 1, :]
        a, b, d = pair[j:k, j:k], pair[j:k, k : k + 1], pair[k : k + 1, k : k + 1]
        scale = 1.0 / (a * d - b * b)
        left = (d * first_row - b * second_row) * scale
        right = (a * second_row - b * first_row) * scale
        later = row > k
        pair = (
            pair
            - jnp.where(later, pair[:, j:k], 0.0) * left
            - jnp.where(later, pair[:, k : k + 1], 0.0) * right
            - jnp.where(row == k, b / a, 0.0) * first_row
        )
    diagonal = jnp.sum(jnp.where(lane == row, pair, 0.0), axis=1, keepdims=True)
    block_inv = (pair / jnp.sqrt(diagonal))[:, size : 2 * size]

    wide_lane = iota((size, n), 1) - start
    inside = (wide_lane >= 0) & (wide_lane < size)
    eye = jnp.where(wide_lane == iota((size, n), 0), 1.0, 0.0)
    done = jnp.dot(
        block_inv, jnp.where(inside, eye, rows), precision=exact_mode, preferred_element_type=jnp.float32
    )
    below = jnp.where(wide_lane >= size, done, 0.0)
    update = lax.dot_general(
        below, done, (((0,), (0,)), ((), ())), precision=exact_mode, preferred_element_type=jnp.float32
    )
    all_row = iota((n, n), 0) - start
    all_lane = iota((n, n), 1) - start
    keep = jnp.where((all_row >= size) & (all_lane >= 0) & (all_lane < size), 0.0, work[...])
    work[...] = keep - update
    work[pl.ds(start, size), :] = done


def gather_kernel(
    ridge_ref, emb_ref, tgt_ref, col_ref, head_ref, all_tgt_ref, work, pair_ref, send, recv
):
    r = lax.axis_index("rows")
    c = lax.axis_index("cols")
    n_rows = lax.axis_size("rows")
    lines = n_rows // PLANE
    line, q = r // PLANE, r % PLANE
    quarter = col_ref.shape[0] // n_rows
    width = col_ref.shape[1]
    head_lines = pl.cdiv(PW, quarter * PLANE)
    x = line * PLANE + (q + 1 - 2 * (q % 2))
    y = line * PLANE + (q + 2) % PLANE
    qx, qy = q + 1 - 2 * (q % 2), (q + 2) % PLANE
    up, down = r + PLANE, r - PLANE
    has_up, has_down = line < lines - 1, line > 0
    core = (r, 1 - c)

    def rows_of(t, who):
        return pl.ds(pl.multiple_of((t * PLANE + who) * quarter, quarter), quarter)

    own = emb_ref.at[pl.ds(pl.multiple_of(c * quarter, quarter), quarter)]

    def remote(src, dst, kind, t, dev):
        return pltpu.make_async_remote_copy(
            src_ref=src, dst_ref=dst, send_sem=send.at[kind, t], recv_sem=recv.at[kind, t],
            device_id=dev, device_id_type=MESH,
        )

    def whole(kind, t, who, dev, first=False):
        dst = col_ref.at[rows_of(t, who)]
        return remote(own if first else dst, dst, kind, t, dev)

    def part(kind, t, who, side, dev, first=False):
        if quarter % 16 == 0:
            rows, cols = quarter // 2, width
        else:
            rows, cols = quarter, width // 2
        down_by, right_by = (side * rows, 0) if rows < quarter else (0, side * cols)
        start = pl.multiple_of((t * PLANE + who) * quarter + down_by, rows)
        dst = col_ref.at[pl.ds(start, rows), pl.ds(right_by, cols)]
        src = dst
        if first:
            start = pl.multiple_of(c * quarter + down_by, rows)
            src = emb_ref.at[pl.ds(start, rows), pl.ds(right_by, cols)]
        return remote(src, dst, kind, t, dev)

    barrier = pltpu.get_barrier_semaphore()
    for dev in ((x, c), (y, c), core):
        pl.semaphore_signal(barrier, inc=1, device_id=dev, device_id_type=MESH)

    @pl.when(has_up)
    def _():
        pl.semaphore_signal(barrier, inc=1, device_id=(up, c), device_id_type=MESH)

    @pl.when(has_down)
    def _():
        pl.semaphore_signal(barrier, inc=1, device_id=(down, c), device_id_type=MESH)

    pl.semaphore_wait(barrier, 3 + jnp.where(has_up, 1, 0) + jnp.where(has_down, 1, 0))

    def send_on(t, first=False):
        part(2, t, q, 0, (x, c), first).start()
        part(3, t, q, 1, (y, c), first).start()
        part(8, t, q, 1, (x, c), first).start()
        part(9, t, q, 0, (y, c), first).start()

    own_copy = pltpu.make_async_copy(own, col_ref.at[rows_of(line, q)], send.at[7, 0])
    tgt_cols = tgt_ref.shape[1]
    own_tgt = all_tgt_ref.at[:, pl.ds(pl.multiple_of(c * tgt_cols, tgt_cols), tgt_cols)]
    tgt_copy = pltpu.make_async_copy(tgt_ref, own_tgt, send.at[7, 1])

    @pl.when(has_up)
    def _():
        whole(0, line, q, (up, c), True).start()

    @pl.when(has_down)
    def _():
        whole(1, line, q, (down, c), True).start()

    send_on(line, True)
    own_copy.start()
    tgt_copy.start()
    tgt_swap = remote(tgt_ref, own_tgt, 6, 0, core)
    tgt_swap.start()

    def ring_stage(t):
        part(2, t, qx, 0, (x, c)).wait_recv()
        part(5, t, qx, 0, (y, c)).start()
        part(3, t, qy, 1, (y, c)).wait_recv()
        part(4, t, qy, 1, (x, c)).start()

    for step in range(1, lines + 1):
        if step < lines:
            @pl.when(line - step >= 0)
            def _(step=step):
                t = line - step
                whole(0, t, q, (up, c)).wait_recv()

                @pl.when(has_up)
                def _():
                    whole(0, t, q, (up, c)).start()

                send_on(t)

            @pl.when(line + step < lines)
            def _(step=step):
                t = line + step
                whole(1, t, q, (down, c)).wait_recv()

                @pl.when(has_down)
                def _():
                    whole(1, t, q, (down, c)).start()

                send_on(t)

        if step == 1:
            ring_stage(line)
        else:
            @pl.when(line - (step - 1) >= 0)
            def _(step=step):
                ring_stage(line - (step - 1))

            @pl.when(line + (step - 1) < lines)
            def _(step=step):
                ring_stage(line + (step - 1))

    opposite = PLANE - 1 - q

    def ring_rest(t):
        part(8, t, qx, 1, (x, c)).wait_recv()
        part(9, t, qy, 0, (y, c)).wait_recv()
        part(4, t, opposite, 1, (x, c)).wait_recv()
        part(5, t, opposite, 0, (y, c)).wait_recv()

    own_copy.wait()
    for t in range(head_lines):
        ring_rest(t)

    block_heads = col_ref.at[pl.ds(0, PW)]
    head_copy = pltpu.make_async_copy(block_heads, pair_ref.at[c], send.at[7, 2])
    head_swap = remote(block_heads, pair_ref.at[c], 6, 1, core)
    head_swap.start()
    head_copy.start()
    head_copy.wait()
    remote(block_heads, pair_ref.at[1 - c], 6, 1, core).wait()
    head_out = pltpu.make_async_copy(pair_ref, head_ref, send.at[7, 0])
    head_out.start()

    n_head = 2 * PW
    heads = pair_ref[...].reshape(n_head, width)
    heads_sq = dot_t(jnp.ones((8, width), jnp.float32), heads * heads)[:1]
    same = iota((n_head, n_head), 0) == iota((n_head, n_head), 1)
    work[...] = head_gaussian(heads, heads, heads_sq) + jnp.where(same, ridge_ref[0], 0.0)
    lax.fori_loop(0, n_head // BLOCK, lambda i, _: (eliminate(work, i, BLOCK), 0)[1], 0)
    lower = iota((n_head, n_head), 1) // BLOCK <= iota((n_head, n_head), 0) // BLOCK
    work[...] = jnp.where(lower, work[...], 0.0)

    for t in range(head_lines, lines):
        ring_rest(t)

    for t in range(lines):
        part(2, t, q, 0, (x, c)).wait_send()
        part(3, t, q, 1, (y, c)).wait_send()
        part(8, t, q, 1, (x, c)).wait_send()
        part(9, t, q, 0, (y, c)).wait_send()
        part(4, t, qy, 1, (x, c)).wait_send()
        part(5, t, qx, 0, (y, c)).wait_send()

        @pl.when(has_up & (t <= line))
        def _(t=t):
            whole(0, t, q, (up, c)).wait_send()

        @pl.when(has_down & (t >= line))
        def _(t=t):
            whole(1, t, q, (down, c)).wait_send()

    tgt_copy.wait()
    head_out.wait()
    other_tgt = all_tgt_ref.at[:, pl.ds(pl.multiple_of((1 - c) * tgt_cols, tgt_cols), tgt_cols)]
    remote(tgt_ref, other_tgt, 6, 0, core).wait()


def gather(ridge_shift, embedded, targets, n_rows):
    width = embedded.shape[1]
    hbm = pl.BlockSpec(memory_space=pl.ANY)
    kinds = (10, max(n_rows // PLANE, 3))
    return pl.pallas_call(
        gather_kernel,
        out_shape=(
            jax.ShapeDtypeStruct((C // 2, width), jnp.float32),
            jax.ShapeDtypeStruct((2, PW, width), jnp.float32),
            jax.ShapeDtypeStruct((targets.shape[0], 2 * targets.shape[1]), jnp.float32),
            jax.ShapeDtypeStruct((2 * PW, 2 * PW), jnp.float32),
        ),
        in_specs=[pl.BlockSpec(memory_space=pltpu.SMEM), hbm, hbm],
        out_specs=(hbm, hbm, hbm, pl.BlockSpec(memory_space=pltpu.VMEM)),
        scratch_shapes=[
            pltpu.VMEM((2, PW, width), jnp.float32),
            pltpu.SemaphoreType.DMA(kinds),
            pltpu.SemaphoreType.DMA(kinds),
        ],
        compiler_params=pltpu.CompilerParams(
            collective_id=0, has_side_effects=True, vmem_limit_bytes=48 * 1024 * 1024
        ),
    )(ridge_shift, embedded, targets)


def finish_kernel(
    ridge_ref, part_ref, emb_ref, col_ref, head_ref, slab_ref, inv_ref, out_ref, panel_ref, rem_ref,
    opp_x, opp_y, from_x, from_y, to_x, to_y, acc, from_down, from_up, land, head_slab, send, recv,
):
    r = lax.axis_index("rows")
    c = lax.axis_index("cols")
    n_rows = lax.axis_size("rows")
    lines = n_rows // PLANE
    line, q = r // PLANE, r % PLANE
    qx, qy = q + 1 - 2 * (q % 2), (q + 2) % PLANE
    opposite = PLANE - 1 - q
    x, y = (line * PLANE + qx, c), (line * PLANE + qy, c)
    up, down = (r + PLANE, c), (r - PLANE, c)
    has_up, has_down = line < lines - 1, line > 0
    wide = part_ref.shape[2]
    half = wide // 2
    lo, hi = pl.ds(0, half), pl.ds(half, half)
    rows_here = emb_ref.shape[0]
    half_cols = col_ref.shape[0]
    quarter = half_cols // n_rows
    n_head = head_ref.shape[0]
    pw = n_head // 2
    ridge = ridge_ref[0]

    def remote(src, dst, kind, t, dev):
        return pltpu.make_async_remote_copy(
            src_ref=src, dst_ref=dst, send_sem=send.at[kind, t], recv_sem=recv.at[kind, t],
            device_id=dev, device_id_type=MESH,
        )

    def c_opp_x(t):
        return remote(part_ref.at[t * PLANE + opposite, :, lo], opp_x.at[t], 0, t, x)

    def c_opp_y(t):
        return remote(part_ref.at[t * PLANE + opposite, :, hi], opp_y.at[t], 1, t, y)

    def c_plain_x(t):
        return remote(part_ref.at[t * PLANE + qx, :, lo], from_x.at[t, :, lo], 2, t, x)

    def c_plain_y(t):
        return remote(part_ref.at[t * PLANE + qy, :, hi], from_y.at[t, :, hi], 3, t, y)

    def c_sum_x(t):
        return remote(to_x.at[t], from_x.at[t, :, hi], 4, t, x)

    def c_sum_y(t):
        return remote(to_y.at[t], from_y.at[t, :, lo], 5, t, y)

    def c_up(t):
        return remote(acc.at[t], from_down.at[t], 6, t, up)

    def c_down(t):
        return remote(acc.at[t], from_up.at[t], 7, t, down)

    barrier = pltpu.get_barrier_semaphore()
    for dev in (x, y):
        pl.semaphore_signal(barrier, inc=1, device_id=dev, device_id_type=MESH)

    @pl.when(has_up)
    def _():
        pl.semaphore_signal(barrier, inc=1, device_id=up, device_id_type=MESH)

    @pl.when(has_down)
    def _():
        pl.semaphore_signal(barrier, inc=1, device_id=down, device_id_type=MESH)

    pl.semaphore_wait(barrier, 2 + jnp.where(has_up, 1, 0) + jnp.where(has_down, 1, 0))

    order = []
    for t in range((lines + 1) // 2):
        order += [t] if t == lines - 1 - t else [t, lines - 1 - t]
    for t in order:
        c_opp_x(t).start()
        c_opp_y(t).start()
    for t in order:
        c_plain_x(t).start()
        c_plain_y(t).start()

    heads = head_ref[...]
    heads_sq = dot_t(jnp.ones((8, heads.shape[1]), jnp.float32), heads * heads)[:1]
    def ring_sum(t):
        c_opp_x(t).wait_recv()
        to_y[t] = part_ref[t * PLANE + qy, :, lo] + opp_x[t]
        c_sum_y(t).start()
        c_opp_y(t).wait_recv()
        to_x[t] = part_ref[t * PLANE + qx, :, hi] + opp_y[t]
        c_sum_x(t).start()

    def ring_total(t):
        c_plain_x(t).wait_recv()
        c_plain_y(t).wait_recv()
        c_sum_x(t).wait_recv()
        c_sum_y(t).wait_recv()
        acc[t] = part_ref[t * PLANE + q] + from_x[t] + from_y[t]

    def line_step(step):
        @pl.when(line <= step)
        def _():
            t = lines - 1 - step + line

            @pl.when(has_down)
            def _():
                c_up(t).wait_recv()
                acc[t] = acc[t] + from_down[t]

            c_up(t).start()

        @pl.when(lines - 1 - line <= step)
        def _():
            t = step - (lines - 1 - line)

            @pl.when(has_up)
            def _():
                c_down(t).wait_recv()
                acc[t] = acc[t] + from_up[t]

            c_down(t).start()

    def line_end():
        out_ref[...] = acc[line]

        @pl.when(has_down)
        def _():
            c_up(line).wait_recv()
            out_ref[...] += from_down[line]

        @pl.when(has_up)
        def _():
            c_down(line).wait_recv()
            out_ref[...] += from_up[line]

    head_row = iota((rows_here, n_head), 0)
    head_col = iota((rows_here, n_head), 1)
    block = head_col // pw
    offset = head_row - block * quarter
    hits = (offset >= 0) & (offset < quarter) & (head_col - block * pw == r * quarter + offset)
    head_slab[...] = head_gaussian(emb_ref[...], heads, heads_sq) + jnp.where(hits, ridge, 0.0)

    chunk = n_head

    def land_chunk(i, _):
        start = pl.multiple_of(i * chunk, chunk)
        row = iota((chunk, n_head), 0) + start
        hit = (row < pw) & (iota((chunk, n_head), 1) == c * pw + row)
        land[pl.ds(start, chunk), :] = head_gaussian(
            col_ref[pl.ds(start, chunk), :], heads, heads_sq
        ) + jnp.where(hit, ridge, 0.0)
        return 0

    lax.fori_loop(0, half_cols // chunk, land_chunk, 0)

    for t in order:
        ring_sum(t)
    inverse = inv_ref[...]
    panels = dot_t(head_slab[...], inverse)
    panel_ref[...] = panels

    def remainder(first):
        rows = dot_t(land[first : first + pw, :], inverse)
        rem_ref[:, first - pw : first] = slab_ref[:, first : first + pw] - dot_t(panels, rows)

    firsts = list(range(pw, half_cols, pw))
    ring_total(order[0])
    if lines > 1:
        ring_total(order[1])
        line_step(0)
    for first in firsts[:2]:
        remainder(first)
    for t in order[2:]:
        ring_total(t)
    if lines > 2:
        line_step(1)
    for first in firsts[2:4]:
        remainder(first)
    if lines > 3:
        line_step(2)
    for first in firsts[4:]:
        remainder(first)
    for step in range(3, lines - 1):
        line_step(step)
    line_end()
    for t in range(lines):
        for copy in (c_opp_x, c_opp_y, c_plain_x, c_plain_y, c_sum_x, c_sum_y):
            copy(t).wait_send()

        @pl.when(t > line)
        def _(t=t):
            c_up(t).wait_send()

        @pl.when(t < line)
        def _(t=t):
            c_down(t).wait_send()


def finish(ridge_shift, partial, embedded, column_emb, heads, kernel_slab, inverse, n_rows):
    lines = n_rows // PLANE
    _, share, wide = partial.shape
    n_head = heads.shape[0]
    rows_here = embedded.shape[0]
    vmem = pl.BlockSpec(memory_space=pltpu.VMEM)
    full = pltpu.VMEM((lines, share, wide), jnp.float32)
    halved = pltpu.VMEM((lines, share, wide // 2), jnp.float32)
    return pl.pallas_call(
        finish_kernel,
        out_shape=(
            jax.ShapeDtypeStruct((share, wide), jnp.float32),
            jax.ShapeDtypeStruct((rows_here, n_head), jnp.float32),
            jax.ShapeDtypeStruct((rows_here, wide - PW), jnp.float32),
        ),
        in_specs=[pl.BlockSpec(memory_space=pltpu.SMEM)] + [vmem] * 6,
        out_specs=(vmem,) * 3,
        scratch_shapes=[
            halved, halved, full, full, halved, halved, full, full, full,
            pltpu.VMEM((wide, n_head), jnp.float32),
            pltpu.VMEM((rows_here, n_head), jnp.float32),
            pltpu.SemaphoreType.DMA((8, lines)),
            pltpu.SemaphoreType.DMA((8, lines)),
        ],
        compiler_params=pltpu.CompilerParams(
            collective_id=1, has_side_effects=True, vmem_limit_bytes=48 * 1024 * 1024
        ),
    )(ridge_shift, partial, embedded, column_emb, heads, kernel_slab, inverse)


def per_device(points, landmark_index, targets, ridge_shift):
    rows_here = landmark_index.shape[0]
    block_points = points.shape[0]
    row_pos = lax.axis_index("rows")
    col_pos = lax.axis_index("cols")
    n_rows = lax.axis_size("rows")
    half_cols = C // 2
    quarter = half_cols // n_rows
    ridge = ridge_shift[0]
    local_index = landmark_index - row_pos * block_points
    embedded = jnp.take(points, local_index, axis=0)
    column_emb, head_pair, all_targets, inverse = gather(ridge_shift, embedded, targets, n_rows)
    heads = head_pair.reshape(2 * PW, -1)

    row_ids = lax.broadcasted_iota(jnp.int32, (rows_here, half_cols), 0)
    col_ids = lax.broadcasted_iota(jnp.int32, (rows_here, half_cols), 1)
    offset = row_ids - col_pos * quarter
    ridge_hits = (offset >= 0) & (offset < quarter) & (col_ids == row_pos * quarter + offset)
    kernel_slab = gaussian(embedded, column_emb) + jnp.where(ridge_hits, ridge, 0.0)
    partial = lax.dot_general(
        all_targets,
        kernel_slab,
        (((0,), (0,)), ((), ())),
        precision=exact_mode,
        preferred_element_type=jnp.float32,
    )
    share = partial.shape[0] // n_rows
    parts = partial.reshape(n_rows, share, half_cols)
    return finish(ridge_shift, parts, embedded, column_emb, heads, kernel_slab, inverse, n_rows)


def solution(mesh):
    in_specs = (P("rows", None), P("rows"), P("rows", "cols"), P())
    out_specs = (P("rows", "cols"), P("rows", None), P("rows", "cols"))
    return jax.shard_map(
        per_device, mesh=mesh, in_specs=in_specs, out_specs=out_specs, check_vma=False
    )
```

```python
import jax
import jax.numpy as jnp
from jax import lax
from jax.experimental import pallas as pl
from jax.experimental.pallas import tpu as pltpu
from jax.sharding import PartitionSpec as P

C = 2048
PW = 128
BLOCK = 32

exact_mode = lax.Precision.HIGHEST


def dot_t(left, right):
    return lax.dot_general(
        left, right, (((1,), (1,)), ((), ())), precision=exact_mode, preferred_element_type=jnp.float32
    )


def gaussian(left_rows, right_rows):
    left_sq = jnp.sum(left_rows * left_rows, axis=1)
    right_sq = jnp.sum(right_rows * right_rows, axis=1)
    cross_term = dot_t(left_rows, right_rows)
    return jnp.exp(
        -(left_sq[:, None] + right_sq[None, :] - 2.0 * cross_term) / (2.0 * left_rows.shape[1])
    )


MESH = pl.DeviceIdType.MESH
PLANE = 4


def head_gaussian(left_rows, heads, heads_sq):
    left_sq = jnp.sum(left_rows * left_rows, axis=1, keepdims=True)
    return jnp.exp(
        -(left_sq + heads_sq - 2.0 * dot_t(left_rows, heads)) / (2.0 * left_rows.shape[1])
    )


def iota(shape, axis):
    return lax.broadcasted_iota(jnp.int32, shape, axis)


def eliminate(work, first, size):
    n = work.shape[0]
    start = pl.multiple_of(first * size, size)
    rows = work[pl.ds(start, size), :]
    rolled = pltpu.roll(rows, n - start, 1)
    lane = iota((size, 128), 1)
    row = iota((size, 128), 0)
    pair = jnp.where(lane < size, rolled[:, :128], jnp.where(lane == row + size, 1.0, 0.0))
    for j in range(0, size, 2):
        k = j + 1
        first_row, second_row = pair[j:k, :], pair[k : k + 1, :]
        a, b, d = pair[j:k, j:k], pair[j:k, k : k + 1], pair[k : k + 1, k : k + 1]
        scale = 1.0 / (a * d - b * b)
        left = (d * first_row - b * second_row) * scale
        right = (a * second_row - b * first_row) * scale
        later = row > k
        pair = (
            pair
            - jnp.where(later, pair[:, j:k], 0.0) * left
            - jnp.where(later, pair[:, k : k + 1], 0.0) * right
            - jnp.where(row == k, b / a, 0.0) * first_row
        )
    diagonal = jnp.sum(jnp.where(lane == row, pair, 0.0), axis=1, keepdims=True)
    block_inv = (pair / jnp.sqrt(diagonal))[:, size : 2 * size]

    wide_lane = iota((size, n), 1) - start
    inside = (wide_lane >= 0) & (wide_lane < size)
    eye = jnp.where(wide_lane == iota((size, n), 0), 1.0, 0.0)
    done = jnp.dot(
        block_inv, jnp.where(inside, eye, rows), precision=exact_mode, preferred_element_type=jnp.float32
    )
    below = jnp.where(wide_lane >= size, done, 0.0)
    update = lax.dot_general(
        below, done, (((0,), (0,)), ((), ())), precision=exact_mode, preferred_element_type=jnp.float32
    )
    all_row = iota((n, n), 0) - start
    all_lane = iota((n, n), 1) - start
    keep = jnp.where((all_row >= size) & (all_lane >= 0) & (all_lane < size), 0.0, work[...])
    work[...] = keep - update
    work[pl.ds(start, size), :] = done


def gather_kernel(
    emb_ref, tgt_ref, col_ref, head_ref, all_tgt_ref, send, recv
):
    r = lax.axis_index("rows")
    c = lax.axis_index("cols")
    n_rows = lax.axis_size("rows")
    lines = n_rows // PLANE
    line, q = r // PLANE, r % PLANE
    quarter = col_ref.shape[0] // n_rows
    width = col_ref.shape[1]
    head_lines = pl.cdiv(PW, quarter * PLANE)
    x = line * PLANE + (q + 1 - 2 * (q % 2))
    y = line * PLANE + (q + 2) % PLANE
    qx, qy = q + 1 - 2 * (q % 2), (q + 2) % PLANE
    up, down = r + PLANE, r - PLANE
    has_up, has_down = line < lines - 1, line > 0
    core = (r, 1 - c)

    def rows_of(t, who):
        return pl.ds(pl.multiple_of((t * PLANE + who) * quarter, quarter), quarter)

    own = emb_ref.at[pl.ds(pl.multiple_of(c * quarter, quarter), quarter)]

    def remote(src, dst, kind, t, dev):
        return pltpu.make_async_remote_copy(
            src_ref=src, dst_ref=dst, send_sem=send.at[kind, t], recv_sem=recv.at[kind, t],
            device_id=dev, device_id_type=MESH,
        )

    def whole(kind, t, who, dev, first=False):
        dst = col_ref.at[rows_of(t, who)]
        return remote(own if first else dst, dst, kind, t, dev)

    def part(kind, t, who, side, dev, first=False):
        if quarter % 16 == 0:
            rows, cols = quarter // 2, width
        else:
            rows, cols = quarter, width // 2
        down_by, right_by = (side * rows, 0) if rows < quarter else (0, side * cols)
        start = pl.multiple_of((t * PLANE + who) * quarter + down_by, rows)
        dst = col_ref.at[pl.ds(start, rows), pl.ds(right_by, cols)]
        src = dst
        if first:
            start = pl.multiple_of(c * quarter + down_by, rows)
            src = emb_ref.at[pl.ds(start, rows), pl.ds(right_by, cols)]
        return remote(src, dst, kind, t, dev)

    barrier = pltpu.get_barrier_semaphore()
    for dev in ((x, c), (y, c), core):
        pl.semaphore_signal(barrier, inc=1, device_id=dev, device_id_type=MESH)

    @pl.when(has_up)
    def _():
        pl.semaphore_signal(barrier, inc=1, device_id=(up, c), device_id_type=MESH)

    @pl.when(has_down)
    def _():
        pl.semaphore_signal(barrier, inc=1, device_id=(down, c), device_id_type=MESH)

    pl.semaphore_wait(barrier, 3 + jnp.where(has_up, 1, 0) + jnp.where(has_down, 1, 0))

    def send_on(t, first=False):
        part(2, t, q, 0, (x, c), first).start()
        part(3, t, q, 1, (y, c), first).start()
        part(8, t, q, 1, (x, c), first).start()
        part(9, t, q, 0, (y, c), first).start()

    own_copy = pltpu.make_async_copy(own, col_ref.at[rows_of(line, q)], send.at[7, 0])
    tgt_cols = tgt_ref.shape[1]
    own_tgt = all_tgt_ref.at[:, pl.ds(pl.multiple_of(c * tgt_cols, tgt_cols), tgt_cols)]
    tgt_copy = pltpu.make_async_copy(tgt_ref, own_tgt, send.at[7, 1])

    @pl.when(has_up)
    def _():
        whole(0, line, q, (up, c), True).start()

    @pl.when(has_down)
    def _():
        whole(1, line, q, (down, c), True).start()

    send_on(line, True)
    own_copy.start()
    tgt_copy.start()
    tgt_swap = remote(tgt_ref, own_tgt, 6, 0, core)
    tgt_swap.start()

    def ring_stage(t):
        part(2, t, qx, 0, (x, c)).wait_recv()
        part(5, t, qx, 0, (y, c)).start()
        part(3, t, qy, 1, (y, c)).wait_recv()
        part(4, t, qy, 1, (x, c)).start()

    for step in range(1, lines + 1):
        if step < lines:
            @pl.when(line - step >= 0)
            def _(step=step):
                t = line - step
                whole(0, t, q, (up, c)).wait_recv()

                @pl.when(has_up)
                def _():
                    whole(0, t, q, (up, c)).start()

                send_on(t)

            @pl.when(line + step < lines)
            def _(step=step):
                t = line + step
                whole(1, t, q, (down, c)).wait_recv()

                @pl.when(has_down)
                def _():
                    whole(1, t, q, (down, c)).start()

                send_on(t)

        if step == 1:
            ring_stage(line)
        else:
            @pl.when(line - (step - 1) >= 0)
            def _(step=step):
                ring_stage(line - (step - 1))

            @pl.when(line + (step - 1) < lines)
            def _(step=step):
                ring_stage(line + (step - 1))

    opposite = PLANE - 1 - q

    def ring_rest(t):
        part(8, t, qx, 1, (x, c)).wait_recv()
        part(9, t, qy, 0, (y, c)).wait_recv()
        part(4, t, opposite, 1, (x, c)).wait_recv()
        part(5, t, opposite, 0, (y, c)).wait_recv()

    own_copy.wait()
    for t in range(head_lines):
        ring_rest(t)

    block_heads = col_ref.at[pl.ds(0, PW)]
    head_copy = pltpu.make_async_copy(block_heads, head_ref.at[c], send.at[7, 2])
    head_swap = remote(block_heads, head_ref.at[c], 6, 1, core)
    head_swap.start()
    head_copy.start()

    for t in range(head_lines, lines):
        ring_rest(t)

    for t in range(lines):
        part(2, t, q, 0, (x, c)).wait_send()
        part(3, t, q, 1, (y, c)).wait_send()
        part(8, t, q, 1, (x, c)).wait_send()
        part(9, t, q, 0, (y, c)).wait_send()
        part(4, t, qy, 1, (x, c)).wait_send()
        part(5, t, qx, 0, (y, c)).wait_send()

        @pl.when(has_up & (t <= line))
        def _(t=t):
            whole(0, t, q, (up, c)).wait_send()

        @pl.when(has_down & (t >= line))
        def _(t=t):
            whole(1, t, q, (down, c)).wait_send()

    tgt_copy.wait()
    head_copy.wait()
    remote(block_heads, head_ref.at[1 - c], 6, 1, core).wait()
    other_tgt = all_tgt_ref.at[:, pl.ds(pl.multiple_of((1 - c) * tgt_cols, tgt_cols), tgt_cols)]
    remote(tgt_ref, other_tgt, 6, 0, core).wait()


def gather(embedded, targets, n_rows):
    width = embedded.shape[1]
    hbm = pl.BlockSpec(memory_space=pl.ANY)
    kinds = (10, max(n_rows // PLANE, 3))
    return pl.pallas_call(
        gather_kernel,
        out_shape=(
            jax.ShapeDtypeStruct((C // 2, width), jnp.float32),
            jax.ShapeDtypeStruct((2, PW, width), jnp.float32),
            jax.ShapeDtypeStruct((targets.shape[0], 2 * targets.shape[1]), jnp.float32),
        ),
        in_specs=[hbm, hbm],
        out_specs=(hbm, hbm, hbm),
        scratch_shapes=[
            pltpu.SemaphoreType.DMA(kinds),
            pltpu.SemaphoreType.DMA(kinds),
        ],
        compiler_params=pltpu.CompilerParams(collective_id=0, has_side_effects=True),
    )(embedded, targets)


def finish_kernel(
    ridge_ref, part_ref, emb_ref, col_ref, head_ref, slab_ref, out_ref, panel_ref, rem_ref,
    opp_x, opp_y, from_x, from_y, to_x, to_y, acc, from_down, from_up, work, land, head_slab, send, recv,
):
    r = lax.axis_index("rows")
    c = lax.axis_index("cols")
    n_rows = lax.axis_size("rows")
    lines = n_rows // PLANE
    line, q = r // PLANE, r % PLANE
    qx, qy = q + 1 - 2 * (q % 2), (q + 2) % PLANE
    opposite = PLANE - 1 - q
    x, y = (line * PLANE + qx, c), (line * PLANE + qy, c)
    up, down = (r + PLANE, c), (r - PLANE, c)
    has_up, has_down = line < lines - 1, line > 0
    wide = part_ref.shape[2]
    half = wide // 2
    lo, hi = pl.ds(0, half), pl.ds(half, half)
    rows_here = emb_ref.shape[0]
    half_cols = col_ref.shape[0]
    quarter = half_cols // n_rows
    n_head = head_ref.shape[0]
    pw = n_head // 2
    ridge = ridge_ref[0]

    def remote(src, dst, kind, t, dev):
        return pltpu.make_async_remote_copy(
            src_ref=src, dst_ref=dst, send_sem=send.at[kind, t], recv_sem=recv.at[kind, t],
            device_id=dev, device_id_type=MESH,
        )

    def c_opp_x(t):
        return remote(part_ref.at[t * PLANE + opposite, :, lo], opp_x.at[t], 0, t, x)

    def c_opp_y(t):
        return remote(part_ref.at[t * PLANE + opposite, :, hi], opp_y.at[t], 1, t, y)

    def c_plain_x(t):
        return remote(part_ref.at[t * PLANE + qx, :, lo], from_x.at[t, :, lo], 2, t, x)

    def c_plain_y(t):
        return remote(part_ref.at[t * PLANE + qy, :, hi], from_y.at[t, :, hi], 3, t, y)

    def c_sum_x(t):
        return remote(to_x.at[t], from_x.at[t, :, hi], 4, t, x)

    def c_sum_y(t):
        return remote(to_y.at[t], from_y.at[t, :, lo], 5, t, y)

    def c_up(t):
        return remote(acc.at[t], from_down.at[t], 6, t, up)

    def c_down(t):
        return remote(acc.at[t], from_up.at[t], 7, t, down)

    barrier = pltpu.get_barrier_semaphore()
    for dev in (x, y):
        pl.semaphore_signal(barrier, inc=1, device_id=dev, device_id_type=MESH)

    @pl.when(has_up)
    def _():
        pl.semaphore_signal(barrier, inc=1, device_id=up, device_id_type=MESH)

    @pl.when(has_down)
    def _():
        pl.semaphore_signal(barrier, inc=1, device_id=down, device_id_type=MESH)

    pl.semaphore_wait(barrier, 2 + jnp.where(has_up, 1, 0) + jnp.where(has_down, 1, 0))

    order = []
    for t in range((lines + 1) // 2):
        order += [t] if t == lines - 1 - t else [t, lines - 1 - t]
    def ring_start(shards):
        for t in shards:
            c_opp_x(t).start()
            c_opp_y(t).start()
        for t in shards:
            c_plain_x(t).start()
            c_plain_y(t).start()

    ends, middle = order[:2], order[2:]
    ring_start(ends)

    heads = head_ref[...]
    heads_sq = dot_t(jnp.ones((8, heads.shape[1]), jnp.float32), heads * heads)[:1]
    same = iota((n_head, n_head), 0) == iota((n_head, n_head), 1)
    work[...] = head_gaussian(heads, heads, heads_sq) + jnp.where(same, ridge, 0.0)
    blocks = n_head // BLOCK

    def factor(first, last):
        step = lambda i, _: (eliminate(work, i, BLOCK), 0)[1]
        lax.fori_loop(blocks * first // 8, blocks * last // 8, step, 0)

    def ring_sum(t):
        c_opp_x(t).wait_recv()
        to_y[t] = part_ref[t * PLANE + qy, :, lo] + opp_x[t]
        c_sum_y(t).start()
        c_opp_y(t).wait_recv()
        to_x[t] = part_ref[t * PLANE + qx, :, hi] + opp_y[t]
        c_sum_x(t).start()

    def ring_total(t):
        c_plain_x(t).wait_recv()
        c_plain_y(t).wait_recv()
        c_sum_x(t).wait_recv()
        c_sum_y(t).wait_recv()
        acc[t] = part_ref[t * PLANE + q] + from_x[t] + from_y[t]

    def line_step(step):
        @pl.when(line <= step)
        def _():
            t = lines - 1 - step + line

            @pl.when(has_down)
            def _():
                c_up(t).wait_recv()
                acc[t] = acc[t] + from_down[t]

            c_up(t).start()

        @pl.when(lines - 1 - line <= step)
        def _():
            t = step - (lines - 1 - line)

            @pl.when(has_up)
            def _():
                c_down(t).wait_recv()
                acc[t] = acc[t] + from_up[t]

            c_down(t).start()

    def line_end():
        out_ref[...] = acc[line]

        @pl.when(has_down)
        def _():
            c_up(line).wait_recv()
            out_ref[...] += from_down[line]

        @pl.when(has_up)
        def _():
            c_down(line).wait_recv()
            out_ref[...] += from_up[line]

    head_row = iota((rows_here, n_head), 0)
    head_col = iota((rows_here, n_head), 1)
    block = head_col // pw
    offset = head_row - block * quarter
    hits = (offset >= 0) & (offset < quarter) & (head_col - block * pw == r * quarter + offset)
    head_slab[...] = head_gaussian(emb_ref[...], heads, heads_sq) + jnp.where(hits, ridge, 0.0)

    chunk = n_head

    def land_chunk(i, _):
        start = pl.multiple_of(i * chunk, chunk)
        row = iota((chunk, n_head), 0) + start
        hit = (row < pw) & (iota((chunk, n_head), 1) == c * pw + row)
        land[pl.ds(start, chunk), :] = head_gaussian(
            col_ref[pl.ds(start, chunk), :], heads, heads_sq
        ) + jnp.where(hit, ridge, 0.0)
        return 0


    for t in ends:
        ring_sum(t)
    ring_start(middle)
    factor(0, 2)
    for t in middle:
        ring_sum(t)
    for t in ends:
        ring_total(t)
    if lines > 1:
        line_step(0)
    factor(2, 4)
    for t in middle:
        ring_total(t)
    if lines > 2:
        line_step(1)
    factor(4, 6)
    if lines > 3:
        line_step(2)
    factor(6, 8)
    for step in range(3, lines - 1):
        line_step(step)
    lax.fori_loop(0, half_cols // chunk, land_chunk, 0)
    lower = iota((n_head, n_head), 1) // BLOCK <= iota((n_head, n_head), 0) // BLOCK
    inverse = jnp.where(lower, work[...], 0.0)
    panels = dot_t(head_slab[...], inverse)
    panel_ref[...] = panels
    for first in range(pw, half_cols, pw):
        rows = dot_t(land[first : first + pw, :], inverse)
        rem_ref[:, first - pw : first] = slab_ref[:, first : first + pw] - dot_t(panels, rows)
    line_end()
    for t in range(lines):
        for copy in (c_opp_x, c_opp_y, c_plain_x, c_plain_y, c_sum_x, c_sum_y):
            copy(t).wait_send()

        @pl.when(t > line)
        def _(t=t):
            c_up(t).wait_send()

        @pl.when(t < line)
        def _(t=t):
            c_down(t).wait_send()


def finish(ridge_shift, partial, embedded, column_emb, heads, kernel_slab, n_rows):
    lines = n_rows // PLANE
    _, share, wide = partial.shape
    n_head = heads.shape[0]
    rows_here = embedded.shape[0]
    vmem = pl.BlockSpec(memory_space=pltpu.VMEM)
    full = pltpu.VMEM((lines, share, wide), jnp.float32)
    halved = pltpu.VMEM((lines, share, wide // 2), jnp.float32)
    return pl.pallas_call(
        finish_kernel,
        out_shape=(
            jax.ShapeDtypeStruct((share, wide), jnp.float32),
            jax.ShapeDtypeStruct((rows_here, n_head), jnp.float32),
            jax.ShapeDtypeStruct((rows_here, wide - PW), jnp.float32),
        ),
        in_specs=[pl.BlockSpec(memory_space=pltpu.SMEM)] + [vmem] * 5,
        out_specs=(vmem,) * 3,
        scratch_shapes=[
            halved, halved, full, full, halved, halved, full, full, full,
            pltpu.VMEM((n_head, n_head), jnp.float32),
            pltpu.VMEM((wide, n_head), jnp.float32),
            pltpu.VMEM((rows_here, n_head), jnp.float32),
            pltpu.SemaphoreType.DMA((8, lines)),
            pltpu.SemaphoreType.DMA((8, lines)),
        ],
        compiler_params=pltpu.CompilerParams(
            collective_id=1, has_side_effects=True, vmem_limit_bytes=48 * 1024 * 1024
        ),
    )(ridge_shift, partial, embedded, column_emb, heads, kernel_slab)


def per_device(points, landmark_index, targets, ridge_shift):
    rows_here = landmark_index.shape[0]
    block_points = points.shape[0]
    row_pos = lax.axis_index("rows")
    col_pos = lax.axis_index("cols")
    n_rows = lax.axis_size("rows")
    half_cols = C // 2
    quarter = half_cols // n_rows
    ridge = ridge_shift[0]
    local_index = landmark_index - row_pos * block_points
    embedded = jnp.take(points, local_index, axis=0)
    column_emb, head_pair, all_targets = gather(embedded, targets, n_rows)
    heads = head_pair.reshape(2 * PW, -1)

    row_ids = lax.broadcasted_iota(jnp.int32, (rows_here, half_cols), 0)
    col_ids = lax.broadcasted_iota(jnp.int32, (rows_here, half_cols), 1)
    offset = row_ids - col_pos * quarter
    ridge_hits = (offset >= 0) & (offset < quarter) & (col_ids == row_pos * quarter + offset)
    kernel_slab = gaussian(embedded, column_emb) + jnp.where(ridge_hits, ridge, 0.0)
    partial = lax.dot_general(
        all_targets,
        kernel_slab,
        (((0,), (0,)), ((), ())),
        precision=exact_mode,
        preferred_element_type=jnp.float32,
    )
    share = partial.shape[0] // n_rows
    parts = partial.reshape(n_rows, share, half_cols)
    return finish(ridge_shift, parts, embedded, column_emb, heads, kernel_slab, n_rows)


def solution(mesh):
    in_specs = (P("rows", None), P("rows"), P("rows", "cols"), P())
    out_specs = (P("rows", "cols"), P("rows", None), P("rows", "cols"))
    return jax.shard_map(
        per_device, mesh=mesh, in_specs=in_specs, out_specs=out_specs, check_vma=False
    )
```

```python
import jax
import jax.numpy as jnp
from jax import lax
from jax.experimental import pallas as pl
from jax.experimental.pallas import tpu as pltpu
from jax.sharding import PartitionSpec as P

C = 2048
PW = 128
BLOCK = 32

exact_mode = lax.Precision.HIGHEST


def dot_t(left, right):
    return lax.dot_general(
        left, right, (((1,), (1,)), ((), ())), precision=exact_mode, preferred_element_type=jnp.float32
    )


def gaussian(left_rows, right_rows):
    left_sq = jnp.sum(left_rows * left_rows, axis=1)
    right_sq = jnp.sum(right_rows * right_rows, axis=1)
    cross_term = dot_t(left_rows, right_rows)
    return jnp.exp(
        -(left_sq[:, None] + right_sq[None, :] - 2.0 * cross_term) / (2.0 * left_rows.shape[1])
    )


MESH = pl.DeviceIdType.MESH
PLANE = 4


def head_gaussian(left_rows, heads, heads_sq):
    left_sq = jnp.sum(left_rows * left_rows, axis=1, keepdims=True)
    return jnp.exp(
        -(left_sq + heads_sq - 2.0 * dot_t(left_rows, heads)) / (2.0 * left_rows.shape[1])
    )


def iota(shape, axis):
    return lax.broadcasted_iota(jnp.int32, shape, axis)


def eliminate(work, first, size):
    n = work.shape[0]
    start = pl.multiple_of(first * size, size)
    rows = work[pl.ds(start, size), :]
    rolled = pltpu.roll(rows, n - start, 1)
    lane = iota((size, 128), 1)
    row = iota((size, 128), 0)
    pair = jnp.where(lane < size, rolled[:, :128], jnp.where(lane == row + size, 1.0, 0.0))
    for j in range(0, size, 2):
        k = j + 1
        first_row, second_row = pair[j:k, :], pair[k : k + 1, :]
        a, b, d = pair[j:k, j:k], pair[j:k, k : k + 1], pair[k : k + 1, k : k + 1]
        scale = 1.0 / (a * d - b * b)
        left = (d * first_row - b * second_row) * scale
        right = (a * second_row - b * first_row) * scale
        later = row > k
        pair = (
            pair
            - jnp.where(later, pair[:, j:k], 0.0) * left
            - jnp.where(later, pair[:, k : k + 1], 0.0) * right
            - jnp.where(row == k, b / a, 0.0) * first_row
        )
    diagonal = jnp.sum(jnp.where(lane == row, pair, 0.0), axis=1, keepdims=True)
    block_inv = (pair / jnp.sqrt(diagonal))[:, size : 2 * size]

    wide_lane = iota((size, n), 1) - start
    inside = (wide_lane >= 0) & (wide_lane < size)
    eye = jnp.where(wide_lane == iota((size, n), 0), 1.0, 0.0)
    done = jnp.dot(
        block_inv, jnp.where(inside, eye, rows), precision=exact_mode, preferred_element_type=jnp.float32
    )
    below = jnp.where(wide_lane >= size, done, 0.0)
    update = lax.dot_general(
        below, done, (((0,), (0,)), ((), ())), precision=exact_mode, preferred_element_type=jnp.float32
    )
    all_row = iota((n, n), 0) - start
    all_lane = iota((n, n), 1) - start
    keep = jnp.where((all_row >= size) & (all_lane >= 0) & (all_lane < size), 0.0, work[...])
    work[...] = keep - update
    work[pl.ds(start, size), :] = done


def gather_kernel(
    emb_ref, tgt_ref, col_ref, head_ref, all_tgt_ref, send, recv
):
    r = lax.axis_index("rows")
    c = lax.axis_index("cols")
    n_rows = lax.axis_size("rows")
    lines = n_rows // PLANE
    line, q = r // PLANE, r % PLANE
    quarter = col_ref.shape[0] // n_rows
    width = col_ref.shape[1]
    head_lines = pl.cdiv(PW, quarter * PLANE)
    x = line * PLANE + (q + 1 - 2 * (q % 2))
    y = line * PLANE + (q + 2) % PLANE
    qx, qy = q + 1 - 2 * (q % 2), (q + 2) % PLANE
    up, down = r + PLANE, r - PLANE
    has_up, has_down = line < lines - 1, line > 0
    core = (r, 1 - c)

    def rows_of(t, who):
        return pl.ds(pl.multiple_of((t * PLANE + who) * quarter, quarter), quarter)

    own = emb_ref.at[pl.ds(pl.multiple_of(c * quarter, quarter), quarter)]

    def remote(src, dst, kind, t, dev):
        return pltpu.make_async_remote_copy(
            src_ref=src, dst_ref=dst, send_sem=send.at[kind, t], recv_sem=recv.at[kind, t],
            device_id=dev, device_id_type=MESH,
        )

    def whole(kind, t, who, dev, first=False):
        dst = col_ref.at[rows_of(t, who)]
        return remote(own if first else dst, dst, kind, t, dev)

    def part(kind, t, who, side, dev, first=False):
        if quarter % 16 == 0:
            rows, cols = quarter // 2, width
        else:
            rows, cols = quarter, width // 2
        down_by, right_by = (side * rows, 0) if rows < quarter else (0, side * cols)
        start = pl.multiple_of((t * PLANE + who) * quarter + down_by, rows)
        dst = col_ref.at[pl.ds(start, rows), pl.ds(right_by, cols)]
        src = dst
        if first:
            start = pl.multiple_of(c * quarter + down_by, rows)
            src = emb_ref.at[pl.ds(start, rows), pl.ds(right_by, cols)]
        return remote(src, dst, kind, t, dev)

    barrier = pltpu.get_barrier_semaphore()
    for dev in ((x, c), (y, c), core):
        pl.semaphore_signal(barrier, inc=1, device_id=dev, device_id_type=MESH)

    @pl.when(has_up)
    def _():
        pl.semaphore_signal(barrier, inc=1, device_id=(up, c), device_id_type=MESH)

    @pl.when(has_down)
    def _():
        pl.semaphore_signal(barrier, inc=1, device_id=(down, c), device_id_type=MESH)

    pl.semaphore_wait(barrier, 3 + jnp.where(has_up, 1, 0) + jnp.where(has_down, 1, 0))

    def send_on(t, first=False):
        part(2, t, q, 0, (x, c), first).start()
        part(3, t, q, 1, (y, c), first).start()
        part(8, t, q, 1, (x, c), first).start()
        part(9, t, q, 0, (y, c), first).start()

    own_copy = pltpu.make_async_copy(own, col_ref.at[rows_of(line, q)], send.at[7, 0])
    tgt_cols = tgt_ref.shape[1]
    own_tgt = all_tgt_ref.at[:, pl.ds(pl.multiple_of(c * tgt_cols, tgt_cols), tgt_cols)]
    tgt_copy = pltpu.make_async_copy(tgt_ref, own_tgt, send.at[7, 1])

    @pl.when(has_up)
    def _():
        whole(0, line, q, (up, c), True).start()

    @pl.when(has_down)
    def _():
        whole(1, line, q, (down, c), True).start()

    send_on(line, True)
    own_copy.start()
    tgt_copy.start()
    tgt_swap = remote(tgt_ref, own_tgt, 6, 0, core)
    tgt_swap.start()

    def ring_stage(t):
        part(2, t, qx, 0, (x, c)).wait_recv()
        part(5, t, qx, 0, (y, c)).start()
        part(3, t, qy, 1, (y, c)).wait_recv()
        part(4, t, qy, 1, (x, c)).start()

    for step in range(1, lines + 1):
        if step < lines:
            @pl.when(line - step >= 0)
            def _(step=step):
                t = line - step
                whole(0, t, q, (up, c)).wait_recv()

                @pl.when(has_up)
                def _():
                    whole(0, t, q, (up, c)).start()

                send_on(t)

            @pl.when(line + step < lines)
            def _(step=step):
                t = line + step
                whole(1, t, q, (down, c)).wait_recv()

                @pl.when(has_down)
                def _():
                    whole(1, t, q, (down, c)).start()

                send_on(t)

        if step == 1:
            ring_stage(line)
        else:
            @pl.when(line - (step - 1) >= 0)
            def _(step=step):
                ring_stage(line - (step - 1))

            @pl.when(line + (step - 1) < lines)
            def _(step=step):
                ring_stage(line + (step - 1))

    opposite = PLANE - 1 - q

    def ring_rest(t):
        part(8, t, qx, 1, (x, c)).wait_recv()
        part(9, t, qy, 0, (y, c)).wait_recv()
        part(4, t, opposite, 1, (x, c)).wait_recv()
        part(5, t, opposite, 0, (y, c)).wait_recv()

    own_copy.wait()
    for t in range(head_lines):
        ring_rest(t)

    block_heads = col_ref.at[pl.ds(0, PW)]
    head_copy = pltpu.make_async_copy(block_heads, head_ref.at[c], send.at[7, 2])
    head_swap = remote(block_heads, head_ref.at[c], 6, 1, core)
    head_swap.start()
    head_copy.start()

    for t in range(head_lines, lines):
        ring_rest(t)

    for t in range(lines):
        part(2, t, q, 0, (x, c)).wait_send()
        part(3, t, q, 1, (y, c)).wait_send()
        part(8, t, q, 1, (x, c)).wait_send()
        part(9, t, q, 0, (y, c)).wait_send()
        part(4, t, qy, 1, (x, c)).wait_send()
        part(5, t, qx, 0, (y, c)).wait_send()

        @pl.when(has_up & (t <= line))
        def _(t=t):
            whole(0, t, q, (up, c)).wait_send()

        @pl.when(has_down & (t >= line))
        def _(t=t):
            whole(1, t, q, (down, c)).wait_send()

    tgt_copy.wait()
    head_copy.wait()
    remote(block_heads, head_ref.at[1 - c], 6, 1, core).wait()
    other_tgt = all_tgt_ref.at[:, pl.ds(pl.multiple_of((1 - c) * tgt_cols, tgt_cols), tgt_cols)]
    remote(tgt_ref, other_tgt, 6, 0, core).wait()


def gather(embedded, targets, n_rows):
    width = embedded.shape[1]
    hbm = pl.BlockSpec(memory_space=pl.ANY)
    kinds = (10, max(n_rows // PLANE, 3))
    return pl.pallas_call(
        gather_kernel,
        out_shape=(
            jax.ShapeDtypeStruct((C // 2, width), jnp.float32),
            jax.ShapeDtypeStruct((2, PW, width), jnp.float32),
            jax.ShapeDtypeStruct((targets.shape[0], 2 * targets.shape[1]), jnp.float32),
        ),
        in_specs=[hbm, hbm],
        out_specs=(hbm, hbm, hbm),
        scratch_shapes=[
            pltpu.SemaphoreType.DMA(kinds),
            pltpu.SemaphoreType.DMA(kinds),
        ],
        compiler_params=pltpu.CompilerParams(collective_id=0, has_side_effects=True),
    )(embedded, targets)


def finish_kernel(
    ridge_ref, part_ref, emb_ref, col_ref, head_ref, slab_ref, out_ref, panel_ref, rem_ref,
    opp_x, opp_y, from_x, from_y, to_x, to_y, acc, from_down, from_up, work, land, head_slab, send, recv,
):
    r = lax.axis_index("rows")
    c = lax.axis_index("cols")
    n_rows = lax.axis_size("rows")
    lines = n_rows // PLANE
    line, q = r // PLANE, r % PLANE
    qx, qy = q + 1 - 2 * (q % 2), (q + 2) % PLANE
    opposite = PLANE - 1 - q
    x, y = (line * PLANE + qx, c), (line * PLANE + qy, c)
    up, down = (r + PLANE, c), (r - PLANE, c)
    has_up, has_down = line < lines - 1, line > 0
    wide = part_ref.shape[2]
    half = wide // 2
    lo, hi = pl.ds(0, half), pl.ds(half, half)
    rows_here = emb_ref.shape[0]
    half_cols = col_ref.shape[0]
    quarter = half_cols // n_rows
    n_head = head_ref.shape[0]
    pw = n_head // 2
    ridge = ridge_ref[0]

    def remote(src, dst, kind, t, dev):
        return pltpu.make_async_remote_copy(
            src_ref=src, dst_ref=dst, send_sem=send.at[kind, t], recv_sem=recv.at[kind, t],
            device_id=dev, device_id_type=MESH,
        )

    def c_opp_x(t):
        return remote(part_ref.at[t * PLANE + opposite, :, lo], opp_x.at[t], 0, t, x)

    def c_opp_y(t):
        return remote(part_ref.at[t * PLANE + opposite, :, hi], opp_y.at[t], 1, t, y)

    def c_plain_x(t):
        return remote(part_ref.at[t * PLANE + qx, :, lo], from_x.at[t, :, lo], 2, t, x)

    def c_plain_y(t):
        return remote(part_ref.at[t * PLANE + qy, :, hi], from_y.at[t, :, hi], 3, t, y)

    def c_sum_x(t):
        return remote(to_x.at[t], from_x.at[t, :, hi], 4, t, x)

    def c_sum_y(t):
        return remote(to_y.at[t], from_y.at[t, :, lo], 5, t, y)

    def c_up(t):
        return remote(acc.at[t], from_down.at[t], 6, t, up)

    def c_down(t):
        return remote(acc.at[t], from_up.at[t], 7, t, down)

    barrier = pltpu.get_barrier_semaphore()
    for dev in (x, y):
        pl.semaphore_signal(barrier, inc=1, device_id=dev, device_id_type=MESH)

    @pl.when(has_up)
    def _():
        pl.semaphore_signal(barrier, inc=1, device_id=up, device_id_type=MESH)

    @pl.when(has_down)
    def _():
        pl.semaphore_signal(barrier, inc=1, device_id=down, device_id_type=MESH)

    pl.semaphore_wait(barrier, 2 + jnp.where(has_up, 1, 0) + jnp.where(has_down, 1, 0))

    order = []
    for t in range((lines + 1) // 2):
        order += [t] if t == lines - 1 - t else [t, lines - 1 - t]
    def ring_start(shards):
        for t in shards:
            c_opp_x(t).start()
            c_opp_y(t).start()
        for t in shards:
            c_plain_x(t).start()
            c_plain_y(t).start()

    ends, middle = order[:2], order[2:]
    ring_start(order)

    heads = head_ref[...]
    heads_sq = dot_t(jnp.ones((8, heads.shape[1]), jnp.float32), heads * heads)[:1]
    same = iota((n_head, n_head), 0) == iota((n_head, n_head), 1)
    work[...] = head_gaussian(heads, heads, heads_sq) + jnp.where(same, ridge, 0.0)
    blocks = n_head // BLOCK

    def factor(first, last):
        step = lambda i, _: (eliminate(work, i, BLOCK), 0)[1]
        lax.fori_loop(blocks * first // 8, blocks * last // 8, step, 0)

    def ring_sum(t):
        c_opp_x(t).wait_recv()
        to_y[t] = part_ref[t * PLANE + qy, :, lo] + opp_x[t]
        c_sum_y(t).start()
        c_opp_y(t).wait_recv()
        to_x[t] = part_ref[t * PLANE + qx, :, hi] + opp_y[t]
        c_sum_x(t).start()

    def ring_total(t):
        c_plain_x(t).wait_recv()
        c_plain_y(t).wait_recv()
        c_sum_x(t).wait_recv()
        c_sum_y(t).wait_recv()
        acc[t] = part_ref[t * PLANE + q] + from_x[t] + from_y[t]

    def line_step(step):
        @pl.when(line <= step)
        def _():
            t = lines - 1 - step + line

            @pl.when(has_down)
            def _():
                c_up(t).wait_recv()
                acc[t] = acc[t] + from_down[t]

            c_up(t).start()

        @pl.when(lines - 1 - line <= step)
        def _():
            t = step - (lines - 1 - line)

            @pl.when(has_up)
            def _():
                c_down(t).wait_recv()
                acc[t] = acc[t] + from_up[t]

            c_down(t).start()

    def line_end():
        out_ref[...] = acc[line]

        @pl.when(has_down)
        def _():
            c_up(line).wait_recv()
            out_ref[...] += from_down[line]

        @pl.when(has_up)
        def _():
            c_down(line).wait_recv()
            out_ref[...] += from_up[line]

    head_row = iota((rows_here, n_head), 0)
    head_col = iota((rows_here, n_head), 1)
    block = head_col // pw
    offset = head_row - block * quarter
    hits = (offset >= 0) & (offset < quarter) & (head_col - block * pw == r * quarter + offset)
    head_slab[...] = head_gaussian(emb_ref[...], heads, heads_sq) + jnp.where(hits, ridge, 0.0)

    chunk = n_head

    def land_chunk(i, _):
        start = pl.multiple_of(i * chunk, chunk)
        row = iota((chunk, n_head), 0) + start
        hit = (row < pw) & (iota((chunk, n_head), 1) == c * pw + row)
        land[pl.ds(start, chunk), :] = head_gaussian(
            col_ref[pl.ds(start, chunk), :], heads, heads_sq
        ) + jnp.where(hit, ridge, 0.0)
        return 0


    lax.fori_loop(0, half_cols // chunk, land_chunk, 0)
    factor(0, 1)
    for t in order:
        ring_sum(t)
    factor(1, 3)
    for t in ends:
        ring_total(t)
    if lines > 1:
        line_step(0)
    factor(3, 4)
    for t in middle:
        ring_total(t)
    if lines > 2:
        line_step(1)
    factor(4, 5)
    if lines > 3:
        line_step(2)
    factor(5, 8)
    for step in range(3, lines - 1):
        line_step(step)
    lower = iota((n_head, n_head), 1) // BLOCK <= iota((n_head, n_head), 0) // BLOCK
    inverse = jnp.where(lower, work[...], 0.0)
    panels = dot_t(head_slab[...], inverse)
    panel_ref[...] = panels
    for first in range(pw, half_cols, pw):
        rows = dot_t(land[first : first + pw, :], inverse)
        rem_ref[:, first - pw : first] = slab_ref[:, first : first + pw] - dot_t(panels, rows)
    line_end()
    for t in range(lines):
        for copy in (c_opp_x, c_opp_y, c_plain_x, c_plain_y, c_sum_x, c_sum_y):
            copy(t).wait_send()

        @pl.when(t > line)
        def _(t=t):
            c_up(t).wait_send()

        @pl.when(t < line)
        def _(t=t):
            c_down(t).wait_send()


def finish(ridge_shift, partial, embedded, column_emb, heads, kernel_slab, n_rows):
    lines = n_rows // PLANE
    _, share, wide = partial.shape
    n_head = heads.shape[0]
    rows_here = embedded.shape[0]
    vmem = pl.BlockSpec(memory_space=pltpu.VMEM)
    full = pltpu.VMEM((lines, share, wide), jnp.float32)
    halved = pltpu.VMEM((lines, share, wide // 2), jnp.float32)
    return pl.pallas_call(
        finish_kernel,
        out_shape=(
            jax.ShapeDtypeStruct((share, wide), jnp.float32),
            jax.ShapeDtypeStruct((rows_here, n_head), jnp.float32),
            jax.ShapeDtypeStruct((rows_here, wide - PW), jnp.float32),
        ),
        in_specs=[pl.BlockSpec(memory_space=pltpu.SMEM)] + [vmem] * 5,
        out_specs=(vmem,) * 3,
        scratch_shapes=[
            halved, halved, full, full, halved, halved, full, full, full,
            pltpu.VMEM((n_head, n_head), jnp.float32),
            pltpu.VMEM((wide, n_head), jnp.float32),
            pltpu.VMEM((rows_here, n_head), jnp.float32),
            pltpu.SemaphoreType.DMA((8, lines)),
            pltpu.SemaphoreType.DMA((8, lines)),
        ],
        compiler_params=pltpu.CompilerParams(
            collective_id=1, has_side_effects=True, vmem_limit_bytes=48 * 1024 * 1024
        ),
    )(ridge_shift, partial, embedded, column_emb, heads, kernel_slab)


def per_device(points, landmark_index, targets, ridge_shift):
    rows_here = landmark_index.shape[0]
    block_points = points.shape[0]
    row_pos = lax.axis_index("rows")
    col_pos = lax.axis_index("cols")
    n_rows = lax.axis_size("rows")
    half_cols = C // 2
    quarter = half_cols // n_rows
    ridge = ridge_shift[0]
    local_index = landmark_index - row_pos * block_points
    embedded = jnp.take(points, local_index, axis=0)
    column_emb, head_pair, all_targets = gather(embedded, targets, n_rows)
    heads = head_pair.reshape(2 * PW, -1)

    row_ids = lax.broadcasted_iota(jnp.int32, (rows_here, half_cols), 0)
    col_ids = lax.broadcasted_iota(jnp.int32, (rows_here, half_cols), 1)
    offset = row_ids - col_pos * quarter
    ridge_hits = (offset >= 0) & (offset < quarter) & (col_ids == row_pos * quarter + offset)
    kernel_slab = gaussian(embedded, column_emb) + jnp.where(ridge_hits, ridge, 0.0)
    partial = lax.dot_general(
        all_targets,
        kernel_slab,
        (((0,), (0,)), ((), ())),
        precision=exact_mode,
        preferred_element_type=jnp.float32,
    )
    share = partial.shape[0] // n_rows
    parts = partial.reshape(n_rows, share, half_cols)
    return finish(ridge_shift, parts, embedded, column_emb, heads, kernel_slab, n_rows)


def solution(mesh):
    in_specs = (P("rows", None), P("rows"), P("rows", "cols"), P())
    out_specs = (P("rows", "cols"), P("rows", None), P("rows", "cols"))
    return jax.shard_map(
        per_device, mesh=mesh, in_specs=in_specs, out_specs=out_specs, check_vma=False
    )
```

```python
import jax
import jax.numpy as jnp
from jax import lax
from jax.experimental import pallas as pl
from jax.experimental.pallas import tpu as pltpu
from jax.sharding import PartitionSpec as P

C = 2048
PW = 128
BLOCK = 32

exact_mode = lax.Precision.HIGHEST


def dot_t(left, right):
    return lax.dot_general(
        left, right, (((1,), (1,)), ((), ())), precision=exact_mode, preferred_element_type=jnp.float32
    )


def gaussian(left_rows, right_rows):
    left_sq = jnp.sum(left_rows * left_rows, axis=1)
    right_sq = jnp.sum(right_rows * right_rows, axis=1)
    cross_term = dot_t(left_rows, right_rows)
    return jnp.exp(
        -(left_sq[:, None] + right_sq[None, :] - 2.0 * cross_term) / (2.0 * left_rows.shape[1])
    )


MESH = pl.DeviceIdType.MESH
PLANE = 4


def head_gaussian(left_rows, heads, heads_sq):
    left_sq = jnp.sum(left_rows * left_rows, axis=1, keepdims=True)
    return jnp.exp(
        -(left_sq + heads_sq - 2.0 * dot_t(left_rows, heads)) / (2.0 * left_rows.shape[1])
    )


def iota(shape, axis):
    return lax.broadcasted_iota(jnp.int32, shape, axis)


def eliminate(work, first, size):
    n = work.shape[0]
    start = pl.multiple_of(first * size, size)
    rows = work[pl.ds(start, size), :]
    rolled = pltpu.roll(rows, n - start, 1)
    lane = iota((size, 128), 1)
    row = iota((size, 128), 0)
    pair = jnp.where(lane < size, rolled[:, :128], jnp.where(lane == row + size, 1.0, 0.0))
    finished, rest = [], pair
    for j in range(size - 1):
        if j and j % 8 == 0:
            finished.append(rest[:8, :])
            rest = rest[8:, :]
        at = j % 8
        column = rest[:, j : j + 1]
        scaled = rest[at : at + 1, :] / rest[at : at + 1, j : j + 1]
        rest = rest - jnp.where(row[: rest.shape[0], :] > at, column, 0.0) * scaled
    pair = jnp.concatenate(finished + [rest], axis=0)
    diagonal = jnp.sum(jnp.where(lane == row, pair, 0.0), axis=1, keepdims=True)
    block_inv = (pair / jnp.sqrt(diagonal))[:, size : 2 * size]

    wide_lane = iota((size, n), 1) - start
    inside = (wide_lane >= 0) & (wide_lane < size)
    eye = jnp.where(wide_lane == iota((size, n), 0), 1.0, 0.0)
    done = jnp.dot(
        block_inv, jnp.where(inside, eye, rows), precision=exact_mode, preferred_element_type=jnp.float32
    )
    below = jnp.where(wide_lane >= size, done, 0.0)
    update = lax.dot_general(
        below, done, (((0,), (0,)), ((), ())), precision=exact_mode, preferred_element_type=jnp.float32
    )
    all_row = iota((n, n), 0) - start
    all_lane = iota((n, n), 1) - start
    keep = jnp.where((all_row >= size) & (all_lane >= 0) & (all_lane < size), 0.0, work[...])
    work[...] = keep - update
    work[pl.ds(start, size), :] = done


def gather_kernel(
    emb_ref, tgt_ref, col_ref, head_ref, all_tgt_ref, send, recv
):
    r = lax.axis_index("rows")
    c = lax.axis_index("cols")
    n_rows = lax.axis_size("rows")
    lines = n_rows // PLANE
    line, q = r // PLANE, r % PLANE
    quarter = col_ref.shape[0] // n_rows
    width = col_ref.shape[1]
    head_lines = pl.cdiv(PW, quarter * PLANE)
    x = line * PLANE + (q + 1 - 2 * (q % 2))
    y = line * PLANE + (q + 2) % PLANE
    qx, qy = q + 1 - 2 * (q % 2), (q + 2) % PLANE
    up, down = r + PLANE, r - PLANE
    has_up, has_down = line < lines - 1, line > 0
    core = (r, 1 - c)

    def rows_of(t, who):
        return pl.ds(pl.multiple_of((t * PLANE + who) * quarter, quarter), quarter)

    own = emb_ref.at[pl.ds(pl.multiple_of(c * quarter, quarter), quarter)]

    def remote(src, dst, kind, t, dev):
        return pltpu.make_async_remote_copy(
            src_ref=src, dst_ref=dst, send_sem=send.at[kind, t], recv_sem=recv.at[kind, t],
            device_id=dev, device_id_type=MESH,
        )

    def whole(kind, t, who, dev, first=False):
        dst = col_ref.at[rows_of(t, who)]
        return remote(own if first else dst, dst, kind, t, dev)

    def part(kind, t, who, side, dev, first=False):
        if quarter % 16 == 0:
            rows, cols = quarter // 2, width
        else:
            rows, cols = quarter, width // 2
        down_by, right_by = (side * rows, 0) if rows < quarter else (0, side * cols)
        start = pl.multiple_of((t * PLANE + who) * quarter + down_by, rows)
        dst = col_ref.at[pl.ds(start, rows), pl.ds(right_by, cols)]
        src = dst
        if first:
            start = pl.multiple_of(c * quarter + down_by, rows)
            src = emb_ref.at[pl.ds(start, rows), pl.ds(right_by, cols)]
        return remote(src, dst, kind, t, dev)

    barrier = pltpu.get_barrier_semaphore()
    for dev in ((x, c), (y, c), core):
        pl.semaphore_signal(barrier, inc=1, device_id=dev, device_id_type=MESH)

    @pl.when(has_up)
    def _():
        pl.semaphore_signal(barrier, inc=1, device_id=(up, c), device_id_type=MESH)

    @pl.when(has_down)
    def _():
        pl.semaphore_signal(barrier, inc=1, device_id=(down, c), device_id_type=MESH)

    pl.semaphore_wait(barrier, 3 + jnp.where(has_up, 1, 0) + jnp.where(has_down, 1, 0))

    def send_on(t, first=False):
        part(2, t, q, 0, (x, c), first).start()
        part(3, t, q, 1, (y, c), first).start()
        part(8, t, q, 1, (x, c), first).start()
        part(9, t, q, 0, (y, c), first).start()

    own_copy = pltpu.make_async_copy(own, col_ref.at[rows_of(line, q)], send.at[7, 0])
    tgt_cols = tgt_ref.shape[1]
    own_tgt = all_tgt_ref.at[:, pl.ds(pl.multiple_of(c * tgt_cols, tgt_cols), tgt_cols)]
    tgt_copy = pltpu.make_async_copy(tgt_ref, own_tgt, send.at[7, 1])

    @pl.when(has_up)
    def _():
        whole(0, line, q, (up, c), True).start()

    @pl.when(has_down)
    def _():
        whole(1, line, q, (down, c), True).start()

    send_on(line, True)
    own_copy.start()
    tgt_copy.start()
    tgt_swap = remote(tgt_ref, own_tgt, 6, 0, core)
    tgt_swap.start()

    def ring_stage(t):
        part(2, t, qx, 0, (x, c)).wait_recv()
        part(5, t, qx, 0, (y, c)).start()
        part(3, t, qy, 1, (y, c)).wait_recv()
        part(4, t, qy, 1, (x, c)).start()

    for step in range(1, lines + 1):
        if step < lines:
            @pl.when(line - step >= 0)
            def _(step=step):
                t = line - step
                whole(0, t, q, (up, c)).wait_recv()

                @pl.when(has_up)
                def _():
                    whole(0, t, q, (up, c)).start()

                send_on(t)

            @pl.when(line + step < lines)
            def _(step=step):
                t = line + step
                whole(1, t, q, (down, c)).wait_recv()

                @pl.when(has_down)
                def _():
                    whole(1, t, q, (down, c)).start()

                send_on(t)

        if step == 1:
            ring_stage(line)
        else:
            @pl.when(line - (step - 1) >= 0)
            def _(step=step):
                ring_stage(line - (step - 1))

            @pl.when(line + (step - 1) < lines)
            def _(step=step):
                ring_stage(line + (step - 1))

    opposite = PLANE - 1 - q

    def ring_rest(t):
        part(8, t, qx, 1, (x, c)).wait_recv()
        part(9, t, qy, 0, (y, c)).wait_recv()
        part(4, t, opposite, 1, (x, c)).wait_recv()
        part(5, t, opposite, 0, (y, c)).wait_recv()

    own_copy.wait()
    for t in range(head_lines):
        ring_rest(t)

    block_heads = col_ref.at[pl.ds(0, PW)]
    head_copy = pltpu.make_async_copy(block_heads, head_ref.at[c], send.at[7, 2])
    head_swap = remote(block_heads, head_ref.at[c], 6, 1, core)
    head_swap.start()
    head_copy.start()

    for t in range(head_lines, lines):
        ring_rest(t)

    for t in range(lines):
        part(2, t, q, 0, (x, c)).wait_send()
        part(3, t, q, 1, (y, c)).wait_send()
        part(8, t, q, 1, (x, c)).wait_send()
        part(9, t, q, 0, (y, c)).wait_send()
        part(4, t, qy, 1, (x, c)).wait_send()
        part(5, t, qx, 0, (y, c)).wait_send()

        @pl.when(has_up & (t <= line))
        def _(t=t):
            whole(0, t, q, (up, c)).wait_send()

        @pl.when(has_down & (t >= line))
        def _(t=t):
            whole(1, t, q, (down, c)).wait_send()

    tgt_copy.wait()
    head_copy.wait()
    remote(block_heads, head_ref.at[1 - c], 6, 1, core).wait()
    other_tgt = all_tgt_ref.at[:, pl.ds(pl.multiple_of((1 - c) * tgt_cols, tgt_cols), tgt_cols)]
    remote(tgt_ref, other_tgt, 6, 0, core).wait()


def gather(embedded, targets, n_rows):
    width = embedded.shape[1]
    hbm = pl.BlockSpec(memory_space=pl.ANY)
    kinds = (10, max(n_rows // PLANE, 3))
    return pl.pallas_call(
        gather_kernel,
        out_shape=(
            jax.ShapeDtypeStruct((C // 2, width), jnp.float32),
            jax.ShapeDtypeStruct((2, PW, width), jnp.float32),
            jax.ShapeDtypeStruct((targets.shape[0], 2 * targets.shape[1]), jnp.float32),
        ),
        in_specs=[hbm, hbm],
        out_specs=(hbm, hbm, hbm),
        scratch_shapes=[
            pltpu.SemaphoreType.DMA(kinds),
            pltpu.SemaphoreType.DMA(kinds),
        ],
        compiler_params=pltpu.CompilerParams(collective_id=0, has_side_effects=True),
    )(embedded, targets)


def finish_kernel(
    ridge_ref, part_ref, emb_ref, col_ref, head_ref, slab_ref, out_ref, panel_ref, rem_ref,
    opp_x, opp_y, from_x, from_y, to_x, to_y, acc, from_down, from_up, work, land, head_slab, send, recv,
):
    r = lax.axis_index("rows")
    c = lax.axis_index("cols")
    n_rows = lax.axis_size("rows")
    lines = n_rows // PLANE
    line, q = r // PLANE, r % PLANE
    qx, qy = q + 1 - 2 * (q % 2), (q + 2) % PLANE
    opposite = PLANE - 1 - q
    x, y = (line * PLANE + qx, c), (line * PLANE + qy, c)
    up, down = (r + PLANE, c), (r - PLANE, c)
    has_up, has_down = line < lines - 1, line > 0
    wide = part_ref.shape[2]
    half = wide // 2
    lo, hi = pl.ds(0, half), pl.ds(half, half)
    rows_here = emb_ref.shape[0]
    half_cols = col_ref.shape[0]
    quarter = half_cols // n_rows
    n_head = head_ref.shape[0]
    pw = n_head // 2
    ridge = ridge_ref[0]

    def remote(src, dst, kind, t, dev):
        return pltpu.make_async_remote_copy(
            src_ref=src, dst_ref=dst, send_sem=send.at[kind, t], recv_sem=recv.at[kind, t],
            device_id=dev, device_id_type=MESH,
        )

    def c_opp_x(t):
        return remote(part_ref.at[t * PLANE + opposite, :, lo], opp_x.at[t], 0, t, x)

    def c_opp_y(t):
        return remote(part_ref.at[t * PLANE + opposite, :, hi], opp_y.at[t], 1, t, y)

    def c_plain_x(t):
        return remote(part_ref.at[t * PLANE + qx, :, lo], from_x.at[t, :, lo], 2, t, x)

    def c_plain_y(t):
        return remote(part_ref.at[t * PLANE + qy, :, hi], from_y.at[t, :, hi], 3, t, y)

    def c_sum_x(t):
        return remote(to_x.at[t], from_x.at[t, :, hi], 4, t, x)

    def c_sum_y(t):
        return remote(to_y.at[t], from_y.at[t, :, lo], 5, t, y)

    def c_up(t):
        return remote(acc.at[t], from_down.at[t], 6, t, up)

    def c_down(t):
        return remote(acc.at[t], from_up.at[t], 7, t, down)

    barrier = pltpu.get_barrier_semaphore()
    for dev in (x, y):
        pl.semaphore_signal(barrier, inc=1, device_id=dev, device_id_type=MESH)

    @pl.when(has_up)
    def _():
        pl.semaphore_signal(barrier, inc=1, device_id=up, device_id_type=MESH)

    @pl.when(has_down)
    def _():
        pl.semaphore_signal(barrier, inc=1, device_id=down, device_id_type=MESH)

    pl.semaphore_wait(barrier, 2 + jnp.where(has_up, 1, 0) + jnp.where(has_down, 1, 0))

    order = []
    for t in range((lines + 1) // 2):
        order += [t] if t == lines - 1 - t else [t, lines - 1 - t]
    def ring_start(shards):
        for t in shards:
            c_opp_x(t).start()
            c_opp_y(t).start()
        for t in shards:
            c_plain_x(t).start()
            c_plain_y(t).start()

    ends, middle = order[:2], order[2:]
    ring_start(order)

    heads = head_ref[...]
    heads_sq = dot_t(jnp.ones((8, heads.shape[1]), jnp.float32), heads * heads)[:1]
    same = iota((n_head, n_head), 0) == iota((n_head, n_head), 1)
    work[...] = head_gaussian(heads, heads, heads_sq) + jnp.where(same, ridge, 0.0)
    blocks = n_head // BLOCK

    def factor(first, last):
        step = lambda i, _: (eliminate(work, i, BLOCK), 0)[1]
        lax.fori_loop(blocks * first // 8, blocks * last // 8, step, 0)

    def ring_sum(t):
        c_opp_x(t).wait_recv()
        to_y[t] = part_ref[t * PLANE + qy, :, lo] + opp_x[t]
        c_sum_y(t).start()
        c_opp_y(t).wait_recv()
        to_x[t] = part_ref[t * PLANE + qx, :, hi] + opp_y[t]
        c_sum_x(t).start()

    def ring_total(t):
        c_plain_x(t).wait_recv()
        c_plain_y(t).wait_recv()
        c_sum_x(t).wait_recv()
        c_sum_y(t).wait_recv()
        acc[t] = part_ref[t * PLANE + q] + from_x[t] + from_y[t]

    def line_step(step):
        @pl.when(line <= step)
        def _():
            t = lines - 1 - step + line

            @pl.when(has_down)
            def _():
                c_up(t).wait_recv()
                acc[t] = acc[t] + from_down[t]

            c_up(t).start()

        @pl.when(lines - 1 - line <= step)
        def _():
            t = step - (lines - 1 - line)

            @pl.when(has_up)
            def _():
                c_down(t).wait_recv()
                acc[t] = acc[t] + from_up[t]

            c_down(t).start()

    def line_end():
        out_ref[...] = acc[line]

        @pl.when(has_down)
        def _():
            c_up(line).wait_recv()
            out_ref[...] += from_down[line]

        @pl.when(has_up)
        def _():
            c_down(line).wait_recv()
            out_ref[...] += from_up[line]

    head_row = iota((rows_here, n_head), 0)
    head_col = iota((rows_here, n_head), 1)
    block = head_col // pw
    offset = head_row - block * quarter
    hits = (offset >= 0) & (offset < quarter) & (head_col - block * pw == r * quarter + offset)
    head_slab[...] = head_gaussian(emb_ref[...], heads, heads_sq) + jnp.where(hits, ridge, 0.0)

    chunk = n_head

    def land_chunk(i, _):
        start = pl.multiple_of(i * chunk, chunk)
        row = iota((chunk, n_head), 0) + start
        hit = (row < pw) & (iota((chunk, n_head), 1) == c * pw + row)
        land[pl.ds(start, chunk), :] = head_gaussian(
            col_ref[pl.ds(start, chunk), :], heads, heads_sq
        ) + jnp.where(hit, ridge, 0.0)
        return 0


    lax.fori_loop(0, half_cols // chunk, land_chunk, 0)
    factor(0, 1)
    for t in order:
        ring_sum(t)
    factor(1, 3)
    for t in ends:
        ring_total(t)
    if lines > 1:
        line_step(0)
    factor(3, 4)
    for t in middle:
        ring_total(t)
    if lines > 2:
        line_step(1)
    factor(4, 5)
    if lines > 3:
        line_step(2)
    factor(5, 8)
    for step in range(3, lines - 1):
        line_step(step)
    lower = iota((n_head, n_head), 1) // BLOCK <= iota((n_head, n_head), 0) // BLOCK
    inverse = jnp.where(lower, work[...], 0.0)
    panels = dot_t(head_slab[...], inverse)
    panel_ref[...] = panels
    for first in range(pw, half_cols, pw):
        rows = dot_t(land[first : first + pw, :], inverse)
        rem_ref[:, first - pw : first] = slab_ref[:, first : first + pw] - dot_t(panels, rows)
    line_end()
    for t in range(lines):
        for copy in (c_opp_x, c_opp_y, c_plain_x, c_plain_y, c_sum_x, c_sum_y):
            copy(t).wait_send()

        @pl.when(t > line)
        def _(t=t):
            c_up(t).wait_send()

        @pl.when(t < line)
        def _(t=t):
            c_down(t).wait_send()


def finish(ridge_shift, partial, embedded, column_emb, heads, kernel_slab, n_rows):
    lines = n_rows // PLANE
    _, share, wide = partial.shape
    n_head = heads.shape[0]
    rows_here = embedded.shape[0]
    vmem = pl.BlockSpec(memory_space=pltpu.VMEM)
    full = pltpu.VMEM((lines, share, wide), jnp.float32)
    halved = pltpu.VMEM((lines, share, wide // 2), jnp.float32)
    return pl.pallas_call(
        finish_kernel,
        out_shape=(
            jax.ShapeDtypeStruct((share, wide), jnp.float32),
            jax.ShapeDtypeStruct((rows_here, n_head), jnp.float32),
            jax.ShapeDtypeStruct((rows_here, wide - PW), jnp.float32),
        ),
        in_specs=[pl.BlockSpec(memory_space=pltpu.SMEM)] + [vmem] * 5,
        out_specs=(vmem,) * 3,
        scratch_shapes=[
            halved, halved, full, full, halved, halved, full, full, full,
            pltpu.VMEM((n_head, n_head), jnp.float32),
            pltpu.VMEM((wide, n_head), jnp.float32),
            pltpu.VMEM((rows_here, n_head), jnp.float32),
            pltpu.SemaphoreType.DMA((8, lines)),
            pltpu.SemaphoreType.DMA((8, lines)),
        ],
        compiler_params=pltpu.CompilerParams(
            collective_id=1, has_side_effects=True, vmem_limit_bytes=48 * 1024 * 1024
        ),
    )(ridge_shift, partial, embedded, column_emb, heads, kernel_slab)


def per_device(points, landmark_index, targets, ridge_shift):
    rows_here = landmark_index.shape[0]
    block_points = points.shape[0]
    row_pos = lax.axis_index("rows")
    col_pos = lax.axis_index("cols")
    n_rows = lax.axis_size("rows")
    half_cols = C // 2
    quarter = half_cols // n_rows
    ridge = ridge_shift[0]
    local_index = landmark_index - row_pos * block_points
    embedded = jnp.take(points, local_index, axis=0)
    column_emb, head_pair, all_targets = gather(embedded, targets, n_rows)
    heads = head_pair.reshape(2 * PW, -1)

    row_ids = lax.broadcasted_iota(jnp.int32, (rows_here, half_cols), 0)
    col_ids = lax.broadcasted_iota(jnp.int32, (rows_here, half_cols), 1)
    offset = row_ids - col_pos * quarter
    ridge_hits = (offset >= 0) & (offset < quarter) & (col_ids == row_pos * quarter + offset)
    kernel_slab = gaussian(embedded, column_emb) + jnp.where(ridge_hits, ridge, 0.0)
    partial = lax.dot_general(
        all_targets,
        kernel_slab,
        (((0,), (0,)), ((), ())),
        precision=exact_mode,
        preferred_element_type=jnp.float32,
    )
    share = partial.shape[0] // n_rows
    parts = partial.reshape(n_rows, share, half_cols)
    return finish(ridge_shift, parts, embedded, column_emb, heads, kernel_slab, n_rows)


def solution(mesh):
    in_specs = (P("rows", None), P("rows"), P("rows", "cols"), P())
    out_specs = (P("rows", "cols"), P("rows", None), P("rows", "cols"))
    return jax.shard_map(
        per_device, mesh=mesh, in_specs=in_specs, out_specs=out_specs, check_vma=False
    )
```

```python
import jax
import jax.numpy as jnp
from jax import lax
from jax.experimental import pallas as pl
from jax.experimental.pallas import tpu as pltpu
from jax.sharding import PartitionSpec as P

C = 2048
PW = 128
BLOCK = 64

exact_mode = lax.Precision.HIGHEST


def dot_t(left, right):
    return lax.dot_general(
        left, right, (((1,), (1,)), ((), ())), precision=exact_mode, preferred_element_type=jnp.float32
    )


def gaussian(left_rows, right_rows):
    left_sq = jnp.sum(left_rows * left_rows, axis=1)
    right_sq = jnp.sum(right_rows * right_rows, axis=1)
    cross_term = dot_t(left_rows, right_rows)
    return jnp.exp(
        -(left_sq[:, None] + right_sq[None, :] - 2.0 * cross_term) / (2.0 * left_rows.shape[1])
    )


MESH = pl.DeviceIdType.MESH
PLANE = 4


def head_gaussian(left_rows, heads, heads_sq):
    left_sq = jnp.sum(left_rows * left_rows, axis=1, keepdims=True)
    return jnp.exp(
        -(left_sq + heads_sq - 2.0 * dot_t(left_rows, heads)) / (2.0 * left_rows.shape[1])
    )


def iota(shape, axis):
    return lax.broadcasted_iota(jnp.int32, shape, axis)


def eliminate(work, first, size):
    n = work.shape[0]
    start = pl.multiple_of(first * size, size)
    rows = work[pl.ds(start, size), :]
    rolled = pltpu.roll(rows, n - start, 1)
    lane = iota((size, 128), 1)
    row = iota((size, 128), 0)
    pair = jnp.where(lane < size, rolled[:, :128], jnp.where(lane == row + size, 1.0, 0.0))
    finished, rest = [], pair
    for j in range(size - 1):
        if j and j % 8 == 0:
            finished.append(rest[:8, :])
            rest = rest[8:, :]
        at = j % 8
        column = rest[:, j : j + 1]
        scaled = rest[at : at + 1, :] / rest[at : at + 1, j : j + 1]
        rest = rest - jnp.where(row[: rest.shape[0], :] > at, column, 0.0) * scaled
    pair = jnp.concatenate(finished + [rest], axis=0)
    diagonal = jnp.sum(jnp.where(lane == row, pair, 0.0), axis=1, keepdims=True)
    block_inv = (pair / jnp.sqrt(diagonal))[:, size : 2 * size]

    wide_lane = iota((size, n), 1) - start
    inside = (wide_lane >= 0) & (wide_lane < size)
    eye = jnp.where(wide_lane == iota((size, n), 0), 1.0, 0.0)
    done = jnp.dot(
        block_inv, jnp.where(inside, eye, rows), precision=exact_mode, preferred_element_type=jnp.float32
    )
    below = jnp.where(wide_lane >= size, done, 0.0)
    update = lax.dot_general(
        below, done, (((0,), (0,)), ((), ())), precision=exact_mode, preferred_element_type=jnp.float32
    )
    all_row = iota((n, n), 0) - start
    all_lane = iota((n, n), 1) - start
    keep = jnp.where((all_row >= size) & (all_lane >= 0) & (all_lane < size), 0.0, work[...])
    work[...] = keep - update
    work[pl.ds(start, size), :] = done


def gather_kernel(
    emb_ref, tgt_ref, col_ref, head_ref, all_tgt_ref, send, recv
):
    r = lax.axis_index("rows")
    c = lax.axis_index("cols")
    n_rows = lax.axis_size("rows")
    lines = n_rows // PLANE
    line, q = r // PLANE, r % PLANE
    quarter = col_ref.shape[0] // n_rows
    width = col_ref.shape[1]
    head_lines = pl.cdiv(PW, quarter * PLANE)
    x = line * PLANE + (q + 1 - 2 * (q % 2))
    y = line * PLANE + (q + 2) % PLANE
    qx, qy = q + 1 - 2 * (q % 2), (q + 2) % PLANE
    up, down = r + PLANE, r - PLANE
    has_up, has_down = line < lines - 1, line > 0
    core = (r, 1 - c)

    def rows_of(t, who):
        return pl.ds(pl.multiple_of((t * PLANE + who) * quarter, quarter), quarter)

    own = emb_ref.at[pl.ds(pl.multiple_of(c * quarter, quarter), quarter)]

    def remote(src, dst, kind, t, dev):
        return pltpu.make_async_remote_copy(
            src_ref=src, dst_ref=dst, send_sem=send.at[kind, t], recv_sem=recv.at[kind, t],
            device_id=dev, device_id_type=MESH,
        )

    def whole(kind, t, who, dev, first=False):
        dst = col_ref.at[rows_of(t, who)]
        return remote(own if first else dst, dst, kind, t, dev)

    def part(kind, t, who, side, dev, first=False):
        if quarter % 16 == 0:
            rows, cols = quarter // 2, width
        else:
            rows, cols = quarter, width // 2
        down_by, right_by = (side * rows, 0) if rows < quarter else (0, side * cols)
        start = pl.multiple_of((t * PLANE + who) * quarter + down_by, rows)
        dst = col_ref.at[pl.ds(start, rows), pl.ds(right_by, cols)]
        src = dst
        if first:
            start = pl.multiple_of(c * quarter + down_by, rows)
            src = emb_ref.at[pl.ds(start, rows), pl.ds(right_by, cols)]
        return remote(src, dst, kind, t, dev)

    barrier = pltpu.get_barrier_semaphore()
    for dev in ((x, c), (y, c), core):
        pl.semaphore_signal(barrier, inc=1, device_id=dev, device_id_type=MESH)

    @pl.when(has_up)
    def _():
        pl.semaphore_signal(barrier, inc=1, device_id=(up, c), device_id_type=MESH)

    @pl.when(has_down)
    def _():
        pl.semaphore_signal(barrier, inc=1, device_id=(down, c), device_id_type=MESH)

    pl.semaphore_wait(barrier, 3 + jnp.where(has_up, 1, 0) + jnp.where(has_down, 1, 0))

    def send_on(t, first=False):
        part(2, t, q, 0, (x, c), first).start()
        part(3, t, q, 1, (y, c), first).start()
        part(8, t, q, 1, (x, c), first).start()
        part(9, t, q, 0, (y, c), first).start()

    own_copy = pltpu.make_async_copy(own, col_ref.at[rows_of(line, q)], send.at[7, 0])
    tgt_cols = tgt_ref.shape[1]
    own_tgt = all_tgt_ref.at[:, pl.ds(pl.multiple_of(c * tgt_cols, tgt_cols), tgt_cols)]
    tgt_copy = pltpu.make_async_copy(tgt_ref, own_tgt, send.at[7, 1])

    @pl.when(has_up)
    def _():
        whole(0, line, q, (up, c), True).start()

    @pl.when(has_down)
    def _():
        whole(1, line, q, (down, c), True).start()

    send_on(line, True)
    own_copy.start()
    tgt_copy.start()
    tgt_swap = remote(tgt_ref, own_tgt, 6, 0, core)
    tgt_swap.start()

    def ring_stage(t):
        part(2, t, qx, 0, (x, c)).wait_recv()
        part(5, t, qx, 0, (y, c)).start()
        part(3, t, qy, 1, (y, c)).wait_recv()
        part(4, t, qy, 1, (x, c)).start()

    for step in range(1, lines + 1):
        if step < lines:
            @pl.when(line - step >= 0)
            def _(step=step):
                t = line - step
                whole(0, t, q, (up, c)).wait_recv()

                @pl.when(has_up)
                def _():
                    whole(0, t, q, (up, c)).start()

                send_on(t)

            @pl.when(line + step < lines)
            def _(step=step):
                t = line + step
                whole(1, t, q, (down, c)).wait_recv()

                @pl.when(has_down)
                def _():
                    whole(1, t, q, (down, c)).start()

                send_on(t)

        if step == 1:
            ring_stage(line)
        else:
            @pl.when(line - (step - 1) >= 0)
            def _(step=step):
                ring_stage(line - (step - 1))

            @pl.when(line + (step - 1) < lines)
            def _(step=step):
                ring_stage(line + (step - 1))

    opposite = PLANE - 1 - q

    def ring_rest(t):
        part(8, t, qx, 1, (x, c)).wait_recv()
        part(9, t, qy, 0, (y, c)).wait_recv()
        part(4, t, opposite, 1, (x, c)).wait_recv()
        part(5, t, opposite, 0, (y, c)).wait_recv()

    own_copy.wait()
    for t in range(head_lines):
        ring_rest(t)

    block_heads = col_ref.at[pl.ds(0, PW)]
    head_copy = pltpu.make_async_copy(block_heads, head_ref.at[c], send.at[7, 2])
    head_swap = remote(block_heads, head_ref.at[c], 6, 1, core)
    head_swap.start()
    head_copy.start()

    for t in range(head_lines, lines):
        ring_rest(t)

    for t in range(lines):
        part(2, t, q, 0, (x, c)).wait_send()
        part(3, t, q, 1, (y, c)).wait_send()
        part(8, t, q, 1, (x, c)).wait_send()
        part(9, t, q, 0, (y, c)).wait_send()
        part(4, t, qy, 1, (x, c)).wait_send()
        part(5, t, qx, 0, (y, c)).wait_send()

        @pl.when(has_up & (t <= line))
        def _(t=t):
            whole(0, t, q, (up, c)).wait_send()

        @pl.when(has_down & (t >= line))
        def _(t=t):
            whole(1, t, q, (down, c)).wait_send()

    tgt_copy.wait()
    head_copy.wait()
    remote(block_heads, head_ref.at[1 - c], 6, 1, core).wait()
    other_tgt = all_tgt_ref.at[:, pl.ds(pl.multiple_of((1 - c) * tgt_cols, tgt_cols), tgt_cols)]
    remote(tgt_ref, other_tgt, 6, 0, core).wait()


def gather(embedded, targets, n_rows):
    width = embedded.shape[1]
    hbm = pl.BlockSpec(memory_space=pl.ANY)
    kinds = (10, max(n_rows // PLANE, 3))
    return pl.pallas_call(
        gather_kernel,
        out_shape=(
            jax.ShapeDtypeStruct((C // 2, width), jnp.float32),
            jax.ShapeDtypeStruct((2, PW, width), jnp.float32),
            jax.ShapeDtypeStruct((targets.shape[0], 2 * targets.shape[1]), jnp.float32),
        ),
        in_specs=[hbm, hbm],
        out_specs=(hbm, hbm, hbm),
        scratch_shapes=[
            pltpu.SemaphoreType.DMA(kinds),
            pltpu.SemaphoreType.DMA(kinds),
        ],
        compiler_params=pltpu.CompilerParams(collective_id=0, has_side_effects=True),
    )(embedded, targets)


def finish_kernel(
    ridge_ref, part_ref, emb_ref, col_ref, head_ref, slab_ref, out_ref, panel_ref, rem_ref,
    opp_x, opp_y, from_x, from_y, to_x, to_y, acc, from_down, from_up, work, land, head_slab, send, recv,
):
    r = lax.axis_index("rows")
    c = lax.axis_index("cols")
    n_rows = lax.axis_size("rows")
    lines = n_rows // PLANE
    line, q = r // PLANE, r % PLANE
    qx, qy = q + 1 - 2 * (q % 2), (q + 2) % PLANE
    opposite = PLANE - 1 - q
    x, y = (line * PLANE + qx, c), (line * PLANE + qy, c)
    up, down = (r + PLANE, c), (r - PLANE, c)
    has_up, has_down = line < lines - 1, line > 0
    wide = part_ref.shape[2]
    half = wide // 2
    lo, hi = pl.ds(0, half), pl.ds(half, half)
    rows_here = emb_ref.shape[0]
    half_cols = col_ref.shape[0]
    quarter = half_cols // n_rows
    n_head = head_ref.shape[0]
    pw = n_head // 2
    ridge = ridge_ref[0]

    def remote(src, dst, kind, t, dev):
        return pltpu.make_async_remote_copy(
            src_ref=src, dst_ref=dst, send_sem=send.at[kind, t], recv_sem=recv.at[kind, t],
            device_id=dev, device_id_type=MESH,
        )

    def c_opp_x(t):
        return remote(part_ref.at[t * PLANE + opposite, :, lo], opp_x.at[t], 0, t, x)

    def c_opp_y(t):
        return remote(part_ref.at[t * PLANE + opposite, :, hi], opp_y.at[t], 1, t, y)

    def c_plain_x(t):
        return remote(part_ref.at[t * PLANE + qx, :, lo], from_x.at[t, :, lo], 2, t, x)

    def c_plain_y(t):
        return remote(part_ref.at[t * PLANE + qy, :, hi], from_y.at[t, :, hi], 3, t, y)

    def c_sum_x(t):
        return remote(to_x.at[t], from_x.at[t, :, hi], 4, t, x)

    def c_sum_y(t):
        return remote(to_y.at[t], from_y.at[t, :, lo], 5, t, y)

    def c_up(t):
        return remote(acc.at[t], from_down.at[t], 6, t, up)

    def c_down(t):
        return remote(acc.at[t], from_up.at[t], 7, t, down)

    barrier = pltpu.get_barrier_semaphore()
    for dev in (x, y):
        pl.semaphore_signal(barrier, inc=1, device_id=dev, device_id_type=MESH)

    @pl.when(has_up)
    def _():
        pl.semaphore_signal(barrier, inc=1, device_id=up, device_id_type=MESH)

    @pl.when(has_down)
    def _():
        pl.semaphore_signal(barrier, inc=1, device_id=down, device_id_type=MESH)

    pl.semaphore_wait(barrier, 2 + jnp.where(has_up, 1, 0) + jnp.where(has_down, 1, 0))

    order = []
    for t in range((lines + 1) // 2):
        order += [t] if t == lines - 1 - t else [t, lines - 1 - t]
    def ring_start(shards):
        for t in shards:
            c_opp_x(t).start()
            c_opp_y(t).start()
        for t in shards:
            c_plain_x(t).start()
            c_plain_y(t).start()

    ends, middle = order[:2], order[2:]
    ring_start(order)

    heads = head_ref[...]
    heads_sq = dot_t(jnp.ones((8, heads.shape[1]), jnp.float32), heads * heads)[:1]
    same = iota((n_head, n_head), 0) == iota((n_head, n_head), 1)
    work[...] = head_gaussian(heads, heads, heads_sq) + jnp.where(same, ridge, 0.0)
    blocks = n_head // BLOCK

    def factor(first, last):
        step = lambda i, _: (eliminate(work, i, BLOCK), 0)[1]
        lax.fori_loop(blocks * first // 8, blocks * last // 8, step, 0)

    def ring_sum(t):
        c_opp_x(t).wait_recv()
        to_y[t] = part_ref[t * PLANE + qy, :, lo] + opp_x[t]
        c_sum_y(t).start()
        c_opp_y(t).wait_recv()
        to_x[t] = part_ref[t * PLANE + qx, :, hi] + opp_y[t]
        c_sum_x(t).start()

    def ring_total(t):
        c_plain_x(t).wait_recv()
        c_plain_y(t).wait_recv()
        c_sum_x(t).wait_recv()
        c_sum_y(t).wait_recv()
        acc[t] = part_ref[t * PLANE + q] + from_x[t] + from_y[t]

    def line_step(step):
        @pl.when(line <= step)
        def _():
            t = lines - 1 - step + line

            @pl.when(has_down)
            def _():
                c_up(t).wait_recv()
                acc[t] = acc[t] + from_down[t]

            c_up(t).start()

        @pl.when(lines - 1 - line <= step)
        def _():
            t = step - (lines - 1 - line)

            @pl.when(has_up)
            def _():
                c_down(t).wait_recv()
                acc[t] = acc[t] + from_up[t]

            c_down(t).start()

    def line_end():
        out_ref[...] = acc[line]

        @pl.when(has_down)
        def _():
            c_up(line).wait_recv()
            out_ref[...] += from_down[line]

        @pl.when(has_up)
        def _():
            c_down(line).wait_recv()
            out_ref[...] += from_up[line]

    head_row = iota((rows_here, n_head), 0)
    head_col = iota((rows_here, n_head), 1)
    block = head_col // pw
    offset = head_row - block * quarter
    hits = (offset >= 0) & (offset < quarter) & (head_col - block * pw == r * quarter + offset)
    head_slab[...] = head_gaussian(emb_ref[...], heads, heads_sq) + jnp.where(hits, ridge, 0.0)

    chunk = n_head

    def land_chunk(i, _):
        start = pl.multiple_of(i * chunk, chunk)
        row = iota((chunk, n_head), 0) + start
        hit = (row < pw) & (iota((chunk, n_head), 1) == c * pw + row)
        land[pl.ds(start, chunk), :] = head_gaussian(
            col_ref[pl.ds(start, chunk), :], heads, heads_sq
        ) + jnp.where(hit, ridge, 0.0)
        return 0


    lax.fori_loop(0, half_cols // chunk, land_chunk, 0)
    factor(0, 1)
    for t in order:
        ring_sum(t)
    factor(1, 3)
    for t in ends:
        ring_total(t)
    if lines > 1:
        line_step(0)
    factor(3, 4)
    for t in middle:
        ring_total(t)
    if lines > 2:
        line_step(1)
    factor(4, 5)
    if lines > 3:
        line_step(2)
    factor(5, 8)
    for step in range(3, lines - 1):
        line_step(step)
    lower = iota((n_head, n_head), 1) // BLOCK <= iota((n_head, n_head), 0) // BLOCK
    inverse = jnp.where(lower, work[...], 0.0)
    panels = dot_t(head_slab[...], inverse)
    panel_ref[...] = panels
    for first in range(pw, half_cols, pw):
        rows = dot_t(land[first : first + pw, :], inverse)
        rem_ref[:, first - pw : first] = slab_ref[:, first : first + pw] - dot_t(panels, rows)
    line_end()
    for t in range(lines):
        for copy in (c_opp_x, c_opp_y, c_plain_x, c_plain_y, c_sum_x, c_sum_y):
            copy(t).wait_send()

        @pl.when(t > line)
        def _(t=t):
            c_up(t).wait_send()

        @pl.when(t < line)
        def _(t=t):
            c_down(t).wait_send()


def finish(ridge_shift, partial, embedded, column_emb, heads, kernel_slab, n_rows):
    lines = n_rows // PLANE
    _, share, wide = partial.shape
    n_head = heads.shape[0]
    rows_here = embedded.shape[0]
    vmem = pl.BlockSpec(memory_space=pltpu.VMEM)
    full = pltpu.VMEM((lines, share, wide), jnp.float32)
    halved = pltpu.VMEM((lines, share, wide // 2), jnp.float32)
    return pl.pallas_call(
        finish_kernel,
        out_shape=(
            jax.ShapeDtypeStruct((share, wide), jnp.float32),
            jax.ShapeDtypeStruct((rows_here, n_head), jnp.float32),
            jax.ShapeDtypeStruct((rows_here, wide - PW), jnp.float32),
        ),
        in_specs=[pl.BlockSpec(memory_space=pltpu.SMEM)] + [vmem] * 5,
        out_specs=(vmem,) * 3,
        scratch_shapes=[
            halved, halved, full, full, halved, halved, full, full, full,
            pltpu.VMEM((n_head, n_head), jnp.float32),
            pltpu.VMEM((wide, n_head), jnp.float32),
            pltpu.VMEM((rows_here, n_head), jnp.float32),
            pltpu.SemaphoreType.DMA((8, lines)),
            pltpu.SemaphoreType.DMA((8, lines)),
        ],
        compiler_params=pltpu.CompilerParams(
            collective_id=1, has_side_effects=True, vmem_limit_bytes=48 * 1024 * 1024
        ),
    )(ridge_shift, partial, embedded, column_emb, heads, kernel_slab)


def per_device(points, landmark_index, targets, ridge_shift):
    rows_here = landmark_index.shape[0]
    block_points = points.shape[0]
    row_pos = lax.axis_index("rows")
    col_pos = lax.axis_index("cols")
    n_rows = lax.axis_size("rows")
    half_cols = C // 2
    quarter = half_cols // n_rows
    ridge = ridge_shift[0]
    local_index = landmark_index - row_pos * block_points
    embedded = jnp.take(points, local_index, axis=0)
    column_emb, head_pair, all_targets = gather(embedded, targets, n_rows)
    heads = head_pair.reshape(2 * PW, -1)

    row_ids = lax.broadcasted_iota(jnp.int32, (rows_here, half_cols), 0)
    col_ids = lax.broadcasted_iota(jnp.int32, (rows_here, half_cols), 1)
    offset = row_ids - col_pos * quarter
    ridge_hits = (offset >= 0) & (offset < quarter) & (col_ids == row_pos * quarter + offset)
    kernel_slab = gaussian(embedded, column_emb) + jnp.where(ridge_hits, ridge, 0.0)
    partial = lax.dot_general(
        all_targets,
        kernel_slab,
        (((0,), (0,)), ((), ())),
        precision=exact_mode,
        preferred_element_type=jnp.float32,
    )
    share = partial.shape[0] // n_rows
    parts = partial.reshape(n_rows, share, half_cols)
    return finish(ridge_shift, parts, embedded, column_emb, heads, kernel_slab, n_rows)


def solution(mesh):
    in_specs = (P("rows", None), P("rows"), P("rows", "cols"), P())
    out_specs = (P("rows", "cols"), P("rows", None), P("rows", "cols"))
    return jax.shard_map(
        per_device, mesh=mesh, in_specs=in_specs, out_specs=out_specs, check_vma=False
    )
```
